128 devices in a mesh: row: 8 (over x, core), col: 16 (over z, y).
Axes of the slice: x: 4, y: 4, z: 4, core: 2. Of those that a mesh axis runs over, the one named last changes fastest.
Arguments:
- density: bfloat16 [6144, 6144], P('row', 'col'), may hold values from -5 to 5
- strips: bfloat16 [16384, 8, 128], P(('row', 'col')), may hold values from -5 to 5
- dest_device: int32 [16384, 1], P(('row', 'col')), may hold values from 0 to 127; in each aligned block of 128 rows (0 to 127, 128 to 255, ...) at most 2 rows name the same one
- atom_slot: int32 [16384], P(('row', 'col')), may hold values from 0 to 95
- block_slot: int32 [16384], P(('row', 'col')), may hold values from 0 to 2
- patterns: int32 [3, 48, 48], replicated, may hold values 0 or 1
Outputs:
- density_next: float32 [6144, 6144], P('row', 'col')
- response_next: float32 [6144, 6144], P('row', 'col')
The draws below stay inside these ranges and needn't reach their ends.
Inputs may be any that keep to these rules, and one draw needn't show every extreme that they name: `dest_device`: of the 128 strips of one device, at most 2 name the same owner, and some owner is named that often.
All inputs are finite; a program needn't handle non-finite values.
Results may differ from the reference program's by a relative error of at most 0.0036.
Values may be sent and summed in bfloat16 or wider, within the bound.
A program may use at most 128 MiB of HBM per device.

```python
import math
import jax
import jax.numpy as jnp
import numpy as np

ORB_BLOCK = 128
ATOM_ORB = 8
NB = 48
STEPS = 2
CAPACITY = 2
M = 6144
TR = 768
TC = 384
ITEMS_DEV = 128
ITEMS = 16384
N_COL = 16
DEVICES = 128


def set_ends(result, own_key, smallest, high):
    longest = result.shape.index(max(result.shape))
    spots = []
    for shift in (0, 1):
        where = [jax.random.randint(jax.random.fold_in(own_key, axis), (), 0, length) for axis, length in enumerate(result.shape)]
        where[longest] = (where[longest] + shift) % result.shape[longest]
        spots.append(tuple(where))
    return result.at[spots[0]].set(smallest).at[spots[1]].set(high)


def steps_of(rng, dims, shards, least, largest):
    def one(position, parts):
        draws = jax.random.uniform(jax.random.fold_in(jax.random.fold_in(rng, 6), position), (parts,), jnp.float32, least / len(shards), largest / len(shards))
        return jnp.repeat(jnp.exp(draws), dims[position] // parts).reshape((-1,) + (1,) * (len(dims) - position - 1))

    factor_of = one(*shards[0])
    for cut in shards[1:]:
        factor_of = factor_of * one(*cut)
    return factor_of


def shared_out(stream_key, own, number, rows, amount, top, reach, slope):
    order = jax.random.permutation(stream_key, amount)
    heavy_load, ordinary = shares(amount, rows * top, reach, slope, True), shares(amount, rows * top, reach, slope, False)
    places = jnp.arange(amount)

    def named(tallies, rotation):
        used = int((tallies > 0).sum())
        fixed = max(1, used // 4)
        passed = fixed + (places - fixed + rotation * (used - fixed)) % max(1, amount - fixed)
        return jnp.zeros((amount,), jnp.int32).at[order[jnp.where(places < fixed, places, passed)]].set(jnp.asarray(tallies, jnp.int32))

    tallies = jnp.where(number % 4 == 0, named(heavy_load, number // 4), named(ordinary, number - number // 4 - 1))
    mixed = jax.random.permutation(jax.random.fold_in(own, 3), amount)
    source_of, sink = mixed[0:amount // 2 * 2:2], mixed[1:amount // 2 * 2:2]
    room = jnp.minimum(tallies[source_of] - 1, reach - tallies[sink]) // 2
    room = jnp.where((source_of == order[0]) | (sink == order[0]) | (tallies[sink] == 0), 0, jnp.maximum(room, 0))
    passed = jax.random.randint(jax.random.fold_in(own, 4), (amount // 2,), 0, 1 << 20) % (room + 1)
    tallies = tallies.at[source_of].add(-passed).at[sink].add(passed)
    labels = jnp.searchsorted(jnp.cumsum(tallies), jnp.arange(rows * top), side="right").astype(jnp.int32)
    listing = labels.reshape(top, rows).T
    listing = listing[jax.random.permutation(jax.random.fold_in(own, 1), rows)]
    rotation = jax.random.randint(jax.random.fold_in(own, 2), (rows, 1), 0, top)
    return jnp.take_along_axis(listing, (jnp.arange(top)[None, :] + rotation) % top, axis=1)


def shares(number_of, total, limit, lean, full):
    portions = [(1 << 20) // math.isqrt(rank ** lean) + 1 for rank in range(1, number_of + 1)]
    largest = limit if full else min(limit, max(-(-total // number_of), total * portions[0] // sum(portions)))
    least = 1 if total - largest >= number_of - 1 else 0
    given, spare = [largest] + [least] * (number_of - 1), total - largest - least * (number_of - 1)
    while spare > 0:
        candidates = [i for i in range(1, number_of) if given[i] < largest] or [i for i in range(1, number_of) if given[i] < limit]
        pool, budget = sum([portions[i] for i in candidates]), spare
        for i in candidates:
            addition = min(limit - given[i], max(1, budget * portions[i] // pool), spare)
            given[i] = given[i] + addition
            spare = spare - addition
    return np.array(given)


def scatter_about(own_key, extent, scale, most, pieces=(), kind=jnp.bfloat16):
    factor_of = steps_of(own_key, extent, pieces, -0.22, 0.18) if pieces else 1.0
    drawn = jax.random.normal(own_key, extent, jnp.float32) * scale * factor_of
    return jnp.minimum(jnp.maximum(drawn, -most), most).astype(kind)


def setup_inputs(seed: int = 0) -> dict:
    key_list = jax.random.split(jax.random.key(seed), 7)
    density = scatter_about(key_list[0], (M, M), 1.0, 5.0, ((0, 8), (1, 16)))
    strips = scatter_about(key_list[1], (ITEMS, ATOM_ORB, ORB_BLOCK), 1.0, 5.0, ((0, 128),))
    dest_device_keys = jax.random.split(jax.random.fold_in(key_list[2], 1), ITEMS // ITEMS_DEV)
    dest_device_turns = jax.random.permutation(jax.random.fold_in(key_list[2], 3), ITEMS // ITEMS_DEV)
    dest_device = jax.vmap(lambda own, number: shared_out(jax.random.fold_in(key_list[2], 2), own, number, ITEMS_DEV, DEVICES, 1, CAPACITY, 2))(dest_device_keys, dest_device_turns).reshape((ITEMS, 1))
    atom_slot = set_ends(jax.random.randint(key_list[3], (ITEMS,), 0, TR // ATOM_ORB), jax.random.fold_in(key_list[3], 1), 0, (TR // ATOM_ORB) - 1).astype(jnp.int32)
    block_slot = set_ends(jax.random.randint(key_list[4], (ITEMS,), 0, NB // N_COL), jax.random.fold_in(key_list[4], 1), 0, (NB // N_COL) - 1).astype(jnp.int32)
    patterns = set_ends((jax.random.randint(key_list[5], (3, NB, NB), 0, 5) < 3).astype(jnp.int32), jax.random.fold_in(key_list[5], 1), 0, 1)
    return dict(density=density, strips=strips, dest_device=dest_device, atom_slot=atom_slot, block_slot=block_slot, patterns=patterns)


def expand(pattern):
    diagonal = jnp.eye(NB, dtype=jnp.int32)
    kept = jnp.maximum(pattern, diagonal).astype(jnp.float32)
    return jnp.repeat(jnp.repeat(kept, ORB_BLOCK, axis=0), ORB_BLOCK, axis=1)

def reference(density, strips, dest_device, atom_slot, block_slot, patterns):
    kept_zero = expand(patterns[0])
    kept_first = expand(patterns[1])
    kept_field = expand(patterns[2])
    targets = dest_device[:, 0]
    atom_rows = targets // N_COL * (TR // ATOM_ORB) + atom_slot
    col_blocks = targets % N_COL * (TC // ORB_BLOCK) + block_slot
    field = jnp.zeros((M // ATOM_ORB, ATOM_ORB, NB, ORB_BLOCK), jnp.float32)
    field = field.at[atom_rows, :, col_blocks, :].add(strips.astype(jnp.float32))
    h_field = field.reshape(M, M)
    linear = (-(kept_field * h_field)).astype(jnp.bfloat16)
    zeroth = density
    inv_root = 1.0 / math.sqrt(M)
    new_zeroth = None
    new_linear = None
    for iteration in range(STEPS):
        square = jnp.dot(zeroth, zeroth, preferred_element_type=jnp.float32)
        crossed = jnp.dot(zeroth, linear, preferred_element_type=jnp.float32) + jnp.dot(linear, zeroth, preferred_element_type=jnp.float32)
        if iteration % 2 == 0:
            new_zeroth = kept_zero * (square * inv_root)
            new_linear = kept_first * (crossed * inv_root)
        else:
            new_zeroth = kept_zero * (2.0 * zeroth.astype(jnp.float32) - square * inv_root)
            new_linear = kept_first * (2.0 * linear.astype(jnp.float32) - crossed * inv_root)
        zeroth = new_zeroth.astype(jnp.bfloat16)
        linear = new_linear.astype(jnp.bfloat16)
    return (new_zeroth, new_linear)
```

```python
import math

import jax
import jax.numpy as jnp
from jax import lax
from jax.sharding import PartitionSpec as P

STEPS = 2
CAPACITY = 2


def tile_kept(patterns, which, row_offset, col_offset, block_rows, block_cols, block_width):
    window = lax.dynamic_slice(patterns[which], (row_offset, col_offset), (block_rows, block_cols))
    global_rows = row_offset + lax.iota(jnp.int32, block_rows)
    global_cols = col_offset + lax.iota(jnp.int32, block_cols)
    diagonal = (global_rows[:, None] == global_cols[None, :]).astype(jnp.int32)
    kept = jnp.maximum(window, diagonal).astype(jnp.float32)
    return jnp.repeat(jnp.repeat(kept, block_width, axis=0), block_width, axis=1)


def products(zeroth, linear):
    col_zero, col_first = (
        lax.all_gather(zeroth, "row", axis=0, tiled=True),
        lax.all_gather(linear, "row", axis=0, tiled=True),
    )
    pieces = (
        lax.all_gather(zeroth, "col", axis=1, tiled=True),
        lax.all_gather(linear, "col", axis=1, tiled=True),
    )
    square = jnp.dot(pieces[0], col_zero, preferred_element_type=jnp.float32)
    left_part = jnp.dot(pieces[0], col_first, preferred_element_type=jnp.float32)
    right_part = jnp.dot(pieces[1], col_zero, preferred_element_type=jnp.float32)
    return (square, left_part + right_part)


def on_device(density, strips, dest_device, atom_slot, block_slot, patterns):
    tile_rows, tile_cols = density.shape
    mesh_rows = lax.axis_size("row")
    mesh_cols = lax.axis_size("col")
    devices = mesh_rows * mesh_cols
    matrix_order = tile_rows * mesh_rows
    atom_width = strips.shape[1]
    block_width = strips.shape[2]
    block_rows = tile_rows // block_width
    block_cols = tile_cols // block_width
    row_offset = lax.axis_index("row") * block_rows
    col_offset = lax.axis_index("col") * block_cols
    kept_zero = tile_kept(patterns, 0, row_offset, col_offset, block_rows, block_cols, block_width)
    kept_first = tile_kept(patterns, 1, row_offset, col_offset, block_rows, block_cols, block_width)
    kept_field = tile_kept(patterns, 2, row_offset, col_offset, block_rows, block_cols, block_width)
    capacity = CAPACITY
    targets = dest_device[:, 0]
    order = lax.iota(jnp.int32, targets.shape[0])
    earlier = (targets[:, None] == targets[None, :]) & (order[None, :] < order[:, None])
    ranking = jnp.sum(earlier.astype(jnp.int32), axis=1)
    position = targets * capacity + ranking
    sent_strips = (
        jnp.zeros((devices * capacity, atom_width, block_width), strips.dtype)
        .at[position]
        .set(strips)
    )
    sent_atoms = jnp.full((devices * capacity,), -1, jnp.int32).at[position].set(atom_slot)
    sent_blocks = jnp.zeros((devices * capacity,), jnp.int32).at[position].set(block_slot)
    arrived = (
        lax.all_to_all(
            sent_strips.reshape(devices, capacity, atom_width, block_width),
            ("row", "col"),
            split_axis=0,
            concat_axis=0,
            tiled=True,
        ),
        lax.all_to_all(
            sent_atoms.reshape(devices, capacity),
            ("row", "col"),
            split_axis=0,
            concat_axis=0,
            tiled=True,
        ),
        lax.all_to_all(
            sent_blocks.reshape(devices, capacity),
            ("row", "col"),
            split_axis=0,
            concat_axis=0,
            tiled=True,
        ),
    )
    recv_strips = arrived[0].reshape(-1, atom_width * block_width)
    recv_atoms = arrived[1].reshape(-1)
    recv_blocks = arrived[2].reshape(-1)
    atoms_here = tile_rows // atom_width
    atom_match = recv_atoms[:, None] == lax.iota(jnp.int32, atoms_here)[None, :]
    block_match = recv_blocks[:, None] == lax.iota(jnp.int32, block_cols)[None, :]
    placing = (
        (atom_match[:, :, None] & block_match[:, None, :])
        .astype(jnp.bfloat16)
        .reshape(-1, atoms_here * block_cols)
    )
    summed = lax.dot_general(
        placing, recv_strips, (((0,), (0,)), ((), ())), preferred_element_type=jnp.float32
    )
    h_field = (
        summed.reshape(atoms_here, block_cols, atom_width, block_width)
        .transpose(0, 2, 1, 3)
        .reshape(tile_rows, tile_cols)
    )
    linear = (-(kept_field * h_field)).astype(jnp.bfloat16)
    zeroth = density
    inv_root = 1.0 / math.sqrt(matrix_order)
    new_zeroth = None
    new_linear = None
    for iteration in range(STEPS):
        square, crossed = products(zeroth, linear)
        if iteration % 2 == 0:
            new_zeroth = kept_zero * (square * inv_root)
            new_linear = kept_first * (crossed * inv_root)
        else:
            new_zeroth = kept_zero * (2.0 * zeroth.astype(jnp.float32) - square * inv_root)
            new_linear = kept_first * (2.0 * linear.astype(jnp.float32) - crossed * inv_root)
        zeroth = new_zeroth.astype(jnp.bfloat16)
        linear = new_linear.astype(jnp.bfloat16)
    return (new_zeroth, new_linear)


def solution(mesh):
    return jax.shard_map(
        on_device,
        mesh=mesh,
        in_specs=(
            P("row", "col"),
            P(("row", "col"), None, None),
            P(("row", "col"), None),
            P(("row", "col")),
            P(("row", "col")),
            P(),
        ),
        out_specs=(P("row", "col"), P("row", "col")),
        check_vma=False,
    )
```

```python
import functools
import math

import jax
import jax.numpy as jnp
from jax import lax
from jax.experimental import pallas as pl
from jax.experimental.pallas import tpu as pltpu
from jax.sharding import PartitionSpec as P

CAPACITY = 2
MESH = pl.DeviceIdType.MESH
BF = jnp.bfloat16
F32 = jnp.float32
TR, TC = 768, 384
KB = 1536
SUB = 192
BLK = 128
PLACE = {2: (0, 0), 1: (0, TC), 3: (1, 0), 0: (1, TC)}
N_COPIES = 200


def local_tile(patterns, which, row_offset, col_offset, block_rows, block_cols, block_width):
    window = lax.dynamic_slice(patterns[which], (row_offset, col_offset), (block_rows, block_cols))
    global_rows = row_offset + lax.iota(jnp.int32, block_rows)
    global_cols = col_offset + lax.iota(jnp.int32, block_cols)
    diagonal = (global_rows[:, None] == global_cols[None, :]).astype(jnp.int32)
    kept = jnp.maximum(window, diagonal).astype(jnp.float32)
    return jnp.repeat(jnp.repeat(kept, block_width, axis=0), block_width, axis=1)


def start_linear(strips, dest_device, atom_slot, block_slot, patterns):
    n, atom_width, width = strips.shape
    devices = lax.axis_size("row") * lax.axis_size("col")
    block_rows, block_cols = TR // width, TC // width
    row_offset = lax.axis_index("row") * block_rows
    col_offset = lax.axis_index("col") * block_cols
    kept_field = local_tile(patterns, 2, row_offset, col_offset, block_rows, block_cols, width)
    targets = dest_device[:, 0]
    order = lax.iota(jnp.int32, n)
    earlier = (targets[:, None] == targets[None, :]) & (order[None, :] < order[:, None])
    ranking = jnp.sum(earlier.astype(jnp.int32), axis=1)
    position = targets * CAPACITY + ranking
    spread = (lax.iota(jnp.int32, devices * CAPACITY)[:, None] == position[None, :]).astype(BF)
    lanes = lax.iota(jnp.int32, width)[None, :]
    tags = jnp.where(
        lanes == 0, atom_slot[:, None] + 1, jnp.where(lanes == 1, block_slot[:, None], 0)
    ).astype(BF)
    rows = jnp.concatenate([strips.reshape(n, atom_width * width), tags], axis=1)
    sent = jnp.dot(spread, rows, preferred_element_type=F32).astype(BF)
    got = lax.all_to_all(
        sent.reshape(devices, CAPACITY, (atom_width + 1) * width),
        ("row", "col"), split_axis=0, concat_axis=0, tiled=True,
    ).reshape(devices * CAPACITY, (atom_width + 1) * width)
    recv_atoms = got[:, atom_width * width].astype(jnp.int32) - 1
    recv_blocks = got[:, atom_width * width + 1].astype(jnp.int32)
    atoms_here = TR // atom_width
    cell = recv_atoms * block_cols + recv_blocks
    placing = (cell[:, None] == lax.iota(jnp.int32, atoms_here * block_cols)[None, :]) & (
        recv_atoms[:, None] >= 0
    )
    summed = lax.dot_general(
        placing.astype(BF), got[:, : atom_width * width], (((0,), (0,)), ((), ())),
        preferred_element_type=F32,
    )
    h_field = (
        summed.reshape(atoms_here, block_cols, atom_width, width)
        .transpose(0, 2, 1, 3)
        .reshape(TR, TC)
    )
    return (-(kept_field * h_field)).astype(BF)


def kernel(
    zero_hbm, first_hbm, patterns, out_zero, out_first,
    a, b, turn, total, part, near, far, send_sem, recv_sem, local_sem,
):
    row, col = lax.axis_index("row"), lax.axis_index("col")
    x, core = row // 2, row % 2
    z, y = col // 4, col % 4

    def at(dx=0, dz=0, dy=0, dc=0):
        nx, nz, ny = (lax.rem(x + dx, 4), lax.rem(z + dz, 4), lax.rem(y + dy, 4))
        return {"row": nx * 2 + lax.rem(core + dc, 2), "col": nz * 4 + ny}

    copies = {}
    locals_ = {}

    def send(name, src, dst, device):
        i = len(copies)
        copy = pltpu.make_async_remote_copy(
            src_ref=src, dst_ref=dst, send_sem=send_sem.at[i], recv_sem=recv_sem.at[i],
            device_id=device, device_id_type=MESH,
        )
        copies[name] = copy
        copy.start()

    def got(*names):
        for name in names:
            copies[name].wait_recv()

    def move(name, src, dst):
        copy = pltpu.make_async_copy(src, dst, local_sem.at[len(locals_)])
        locals_[name] = copy
        copy.start()

    def lanes(position):
        return pl.ds(pl.multiple_of(position * TC, BLK), TC)

    def rows_of(position, first=0, size=SUB):
        return pl.ds(pl.multiple_of(core * TR + position * SUB + first, 32), size)

    peers = [at(dy=1), at(dy=3), at(dx=1), at(dx=2), at(dx=3), at(dz=1), at(dz=2), at(dz=3), at(dc=1)]

    def tile(u, rows=slice(None)):
        return a.at[u, rows, lanes(y)]

    def begin_turn(u):
        for dx in (2, 1, 3):
            q = lax.rem(x + dx, 4)
            src = tile(u, pl.ds(pl.multiple_of(q * SUB, 32), SUB))
            send(("tx", u, dx), src, turn.at[u, (4 - dx) % 4], at(dx=dx))
        move(("tx", u), tile(u, pl.ds(pl.multiple_of(x * SUB, 32), SUB)), turn.at[u, 0])

    def begin_side(u):
        send(("y", u, 1), tile(u), tile(u), at(dy=1))
        send(("y", u, 3), tile(u), tile(u), at(dy=3))

    def turn_z(u):
        got(*(("tx", u, dx) for dx in (1, 2, 3)))
        locals_["tx", u].wait()
        for dz in (2, 3, 1, 0):
            chunk, lane = PLACE[(4 - dz) % 4]
            src = turn.at[u, lax.rem(z + dz + 4 - x, 4)]
            dst = b.at[u, chunk, rows_of(x), pl.ds(lane, TC)]
            if dz:
                send(("tz", u, dz), src, dst, at(dz=dz))
            else:
                move(("tz", u), src, dst)

    def spread_own(u, ch):
        if ch == 0:
            got(("tz", u, 2), ("tz", u, 3))
        else:
            got(("tz", u, 1))
            locals_["tz", u].wait()
        own = b.at[u, ch, rows_of(x)]
        send(("x", u, ch, 1), own, own, at(dx=1))
        send(("x", u, ch, 3), own, own, at(dx=3))
        send(("c", u, ch, 0), own, own, at(dc=1))

    def side_on(u):
        half = TR // 2
        got(("y", u, 1))
        src = a.at[u, pl.ds(0, half), lanes(lax.rem(y + 3, 4))]
        send(("yy", u, 1), src, src, at(dy=1))
        got(("y", u, 3))
        src = a.at[u, pl.ds(half, half), lanes(lax.rem(y + 1, 4))]
        send(("yy", u, 3), src, src, at(dy=3))

    def spread_on(u, ch):
        before, after = lax.rem(x + 3, 4), lax.rem(x + 1, 4)
        got(("x", u, ch, 1))
        src = b.at[u, ch, rows_of(before, 0, SUB // 2)]
        send(("xx", u, ch, 1), src, src, at(dx=1))
        src = b.at[u, ch, rows_of(before)]
        send(("c", u, ch, 1), src, src, at(dc=1))
        got(("x", u, ch, 3))
        src = b.at[u, ch, rows_of(after, SUB // 2, SUB // 2)]
        send(("xx", u, ch, 3), src, src, at(dx=3))
        src = b.at[u, ch, rows_of(after)]
        send(("c", u, ch, 3), src, src, at(dc=1))

    def spread_last(u, ch):
        across = lax.rem(x + 2, 4)
        got(("xx", u, ch, 1))
        src = b.at[u, ch, rows_of(across, 0, SUB // 2)]
        send(("c", u, ch, 2), src, src, at(dc=1))
        got(("xx", u, ch, 3))
        src = b.at[u, ch, rows_of(across, SUB // 2, SUB // 2)]
        send(("c", u, ch, 4), src, src, at(dc=1))

    def side_ready(u):
        got(("yy", u, 1), ("yy", u, 3))

    def chunk_ready(u, ch):
        got(*(("c", u, ch, i) for i in range(5)))

    def multiply(p, left, right, ch, add=False):
        @pl.loop(0, 3)
        def _(n):
            cols = pl.ds(pl.multiple_of(n * 256, 256), 256)
            value = jnp.dot(a[left], b[right, ch, :, cols], preferred_element_type=F32)
            if add:
                total[p, ch, :, cols] += value
            else:
                total[p, ch, :, cols] = value

    half = TR // 2

    def sum_far(r, p):
        part[r, 1] = total[p, 0, :, 0:TC].astype(BF)
        send(("s2", r, 1), part.at[r, 1, pl.ds(0, half)], far.at[r, 0], at(dz=1))
        send(("s2", r, 3), part.at[r, 1, pl.ds(half, half)], far.at[r, 1], at(dz=3))

    def sum_up(r, p):
        got(("s2", r, 1))
        part[r, 0, 0:half] = (total[p, 0, 0:half, TC:] + far[r, 0].astype(F32)).astype(BF)
        part[r, 0, half:] = total[p, 0, half:, TC:].astype(BF)
        send(("s1", r, 1), part.at[r, 0], near.at[r, 0], at(dz=1))

    def sum_down(r, p):
        got(("s2", r, 3))
        part[r, 2, 0:half] = total[p, 1, 0:half, 0:TC].astype(BF)
        part[r, 2, half:] = (total[p, 1, half:, 0:TC] + far[r, 1].astype(F32)).astype(BF)
        send(("s1", r, 3), part.at[r, 2], near.at[r, 1], at(dz=3))

    inv_root = 1.0 / math.sqrt(6144)

    def finish(r, p, which, old, write):
        got(("s1", r, 1), ("s1", r, 3))

        @pl.loop(0, TR // BLK)
        def _(i):
            rows = pl.ds(pl.multiple_of(i * BLK, BLK), BLK)
            for j in range(TC // BLK):
                cs = slice(j * BLK, (j + 1) * BLK)
                big_row, big_col = row * (TR // BLK) + i, col * (TC // BLK) + j
                keep = jnp.where(big_row == big_col, 1, patterns[which, big_row, big_col]).astype(F32)
                value = (
                    total[p, 1, rows, TC + j * BLK : TC + (j + 1) * BLK]
                    + near[r, 0, rows, cs].astype(F32)
                    + near[r, 1, rows, cs].astype(F32)
                ) * inv_root
                if old is not None:
                    mine = pl.ds(pl.multiple_of(y * TC + j * BLK, BLK), BLK)
                    value = 2.0 * a[old, rows, mine].astype(F32) - value
                write(rows, j, keep * value)

    def to_unit(u):
        def write(rows, j, value):
            a[u, rows, pl.ds(pl.multiple_of(y * TC + j * BLK, BLK), BLK)] = value.astype(BF)
        return write

    def to_out(ref):
        def write(rows, j, value):
            ref[rows, j * BLK : (j + 1) * BLK] = value
        return write

    move("zero", zero_hbm, tile(0))
    move("first", first_hbm, tile(1))
    barrier = pltpu.get_barrier_semaphore()
    for peer in peers:
        pl.semaphore_signal(barrier, inc=1, device_id=peer, device_id_type=MESH)
    pl.semaphore_wait(barrier, len(peers))

    locals_["zero"].wait()
    begin_turn(0)
    begin_side(0)
    turn_z(0)
    spread_own(0, 0)
    spread_own(0, 1)
    locals_["first"].wait()
    begin_turn(1)
    side_on(0)
    begin_side(1)
    spread_on(0, 0)
    spread_on(0, 1)
    turn_z(1)
    spread_last(0, 0)
    spread_last(0, 1)
    spread_own(1, 0)
    spread_own(1, 1)
    side_ready(0)
    chunk_ready(0, 0)
    multiply(0, 0, 0, 0)
    sum_far(0, 0)
    chunk_ready(0, 1)
    multiply(0, 0, 0, 1)
    side_on(1)
    sum_up(0, 0)
    sum_down(0, 0)
    side_ready(1)
    spread_on(1, 0)
    spread_on(1, 1)
    multiply(1, 1, 0, 0)
    multiply(1, 1, 0, 1)
    spread_last(1, 0)
    spread_last(1, 1)
    finish(0, 0, 0, None, to_unit(2))
    begin_turn(2)
    begin_side(2)
    chunk_ready(1, 0)
    multiply(1, 0, 1, 0, add=True)
    sum_far(1, 1)
    chunk_ready(1, 1)
    multiply(1, 0, 1, 1, add=True)
    turn_z(2)
    sum_up(1, 1)
    sum_down(1, 1)
    side_on(2)
    spread_own(2, 0)
    spread_own(2, 1)
    finish(1, 1, 1, None, to_unit(3))
    begin_turn(3)
    begin_side(3)
    spread_on(2, 0)
    spread_on(2, 1)
    spread_last(2, 0)
    spread_last(2, 1)
    turn_z(3)
    spread_own(3, 0)
    spread_own(3, 1)
    side_ready(2)
    chunk_ready(2, 0)
    multiply(0, 2, 2, 0)
    sum_far(2, 0)
    chunk_ready(2, 1)
    multiply(0, 2, 2, 1)
    side_on(3)
    sum_up(2, 0)
    sum_down(2, 0)
    side_ready(3)
    spread_on(3, 0)
    spread_on(3, 1)
    multiply(1, 3, 2, 0)
    multiply(1, 3, 2, 1)
    spread_last(3, 0)
    spread_last(3, 1)
    chunk_ready(3, 0)
    multiply(1, 2, 3, 0, add=True)
    sum_far(3, 1)
    chunk_ready(3, 1)
    multiply(1, 2, 3, 1, add=True)
    sum_up(3, 1)
    sum_down(3, 1)
    finish(2, 0, 0, 2, to_out(out_zero))
    finish(3, 1, 1, 3, to_out(out_first))
    for copy in copies.values():
        copy.wait_send()


def on_device(density, strips, dest_device, atom_slot, block_slot, patterns):
    linear = start_linear(strips, dest_device, atom_slot, block_slot, patterns)
    out = jax.ShapeDtypeStruct((TR, TC), F32)
    return tuple(pl.pallas_call(
        kernel,
        out_shape=(out, out),
        in_specs=[
            pl.BlockSpec(memory_space=pl.ANY),
            pl.BlockSpec(memory_space=pl.ANY),
            pl.BlockSpec(memory_space=pltpu.SMEM),
        ],
        out_specs=(pl.BlockSpec(memory_space=pltpu.VMEM),) * 2,
        scratch_shapes=[
            pltpu.VMEM((4, TR, KB), BF),
            pltpu.VMEM((4, 2, KB, 2 * TC), BF),
            pltpu.VMEM((4, 4, SUB, TC), BF),
            pltpu.VMEM((2, 2, TR, 2 * TC), F32),
            pltpu.VMEM((4, 3, TR, TC), BF),
            pltpu.VMEM((4, 2, TR, TC), BF),
            pltpu.VMEM((4, 2, TR // 2, TC), BF),
            pltpu.SemaphoreType.DMA((N_COPIES,)),
            pltpu.SemaphoreType.DMA((N_COPIES,)),
            pltpu.SemaphoreType.DMA((16,)),
        ],
        compiler_params=pltpu.CompilerParams(
            collective_id=0, has_side_effects=True, vmem_limit_bytes=62 * 2**20 - 2**19
        ),
        cost_estimate=pl.CostEstimate(flops=21743271936, bytes_accessed=8 * 2**20, transcendentals=0),
    )(density, linear, patterns))


def solution(mesh):
    return jax.shard_map(
        on_device,
        mesh=mesh,
        in_specs=(
            P("row", "col"),
            P(("row", "col"), None, None),
            P(("row", "col"), None),
            P(("row", "col")),
            P(("row", "col")),
            P(),
        ),
        out_specs=(P("row", "col"), P("row", "col")),
        check_vma=False,
    )
```

```python
import math

import jax
import jax.numpy as jnp
from jax import lax
from jax.experimental import pallas as pl
from jax.experimental.pallas import tpu as pltpu
from jax.sharding import PartitionSpec as P

MESH = pl.DeviceIdType.MESH
BF = jnp.bfloat16
F32 = jnp.float32
I32 = jnp.int32
TR, TC = 768, 384
HALF = TR // 2
KB = 1536
SUB = TR // 4
BLK = 128
ATOM = 8
ITEMS = 128
SLOTS = 256
WIDE = ATOM * BLK + BLK
ATOMS = TR // ATOM
N_COPIES = 224


def kernel(
    zero_hbm, strips, dest, atoms, blocks, patterns, out_zero, out_first,
    a, b, turn, total, part, near, far, rows, sent, came, placed, send_sem, recv_sem, local_sem,
):
    row, col = lax.axis_index("row"), lax.axis_index("col")
    x, core = row // 2, row % 2
    z, y = col // 4, col % 4

    def at(dx=0, dz=0, dy=0, dc=0):
        nx, nz, ny = (lax.rem(x + dx, 4), lax.rem(z + dz, 4), lax.rem(y + dy, 4))
        return {"row": nx * 2 + lax.rem(core + dc, 2), "col": nz * 4 + ny}

    copies, moves = {}, {}
    arrived, left = set(), set()

    def send(name, src, dst, device):
        i = len(copies)
        copies[name] = pltpu.make_async_remote_copy(
            src_ref=src, dst_ref=dst, send_sem=send_sem.at[i], recv_sem=recv_sem.at[i],
            device_id=device, device_id_type=MESH,
        )
        copies[name].start()

    def move(name, src, dst):
        moves[name] = pltpu.make_async_copy(src, dst, local_sem.at[len(moves)])
        moves[name].start()

    def got(*names):
        for name in names:
            if name not in arrived:
                arrived.add(name)
                if name in copies:
                    copies[name].wait_recv()
                else:
                    moves[name].wait()

    def gone(*names):
        for name in names:
            if name not in left:
                left.add(name)
                copies[name].wait_send()

    def lanes(position):
        return pl.ds(pl.multiple_of(position * TC, BLK), TC)

    def rows_of(position, first=0, size=SUB):
        return pl.ds(pl.multiple_of(core * TR + position * SUB + first, 32), size)

    def rows_at(position, size):
        return pl.ds(pl.multiple_of(position * size, 32), size)

    def tile(u, where=slice(None)):
        return a.at[u, where, lanes(y)]

    def begin_turn(u):
        if u == 0:
            got("zero")
        for dx in (2, 1, 3):
            src = tile(u, rows_at(lax.rem(x + dx, 4), SUB))
            send(("tx", u, dx), src, turn.at[u, 4 - dx], at(dx=dx))
        move(("t0", u), tile(u, rows_at(x, SUB)), turn.at[u, 0])

    def turn_z(u):
        got(("tx", u, 2), ("tx", u, 1), ("tx", u, 3), ("t0", u))
        for dz in (2, 3, 1, 0):
            src = turn.at[u, lax.rem(z + dz + 4 - x, 4)]
            dst = b.at[u, (4 - dz) % 4, rows_of(x)]
            if dz:
                send(("tz", u, 4 - dz), src, dst, at(dz=dz))
            else:
                move(("tz", u, 0), src, dst)

    def own(u, k):
        got(("tz", u, k))
        src = b.at[u, k, rows_of(x)]
        send(("x", u, k, 1), src, src, at(dx=1))
        send(("x", u, k, 3), src, src, at(dx=3))
        send(("c", u, k, 0), src, src, at(dc=1))

    def fwd(u, k, h):
        got(("x", u, k, h))
        source = lax.rem(x + 4 - h, 4)
        src = b.at[u, k, rows_of(source, SUB // 2 if h == 3 else 0, SUB // 2)]
        send(("xx", u, k, h), src, src, at(dx=h))
        src = b.at[u, k, rows_of(source)]
        send(("c", u, k, h), src, src, at(dc=1))

    def last(u, k, h):
        got(("xx", u, k, h))
        src = b.at[u, k, rows_of(lax.rem(x + 2, 4), SUB // 2 if h == 3 else 0, SUB // 2)]
        send(("c", u, k, h + 1), src, src, at(dc=1))

    def begin_side(u):
        send(("y", u, 1), tile(u), tile(u), at(dy=1))
        send(("y", u, 3), tile(u), tile(u), at(dy=3))

    def side_on(u, h):
        got(("y", u, h))
        where = pl.ds(HALF if h == 3 else 0, HALF)
        src = a.at[u, where, lanes(lax.rem(y + 4 - h, 4))]
        send(("yy", u, h), src, src, at(dy=h))

    def product(left_unit, right_unit, k):
        got(("y", left_unit, 1), ("y", left_unit, 3), ("yy", left_unit, 1), ("yy", left_unit, 3))
        got(("tz", right_unit, k), *(("c", right_unit, k, i) for i in range(5)))
        for h in (1, 3):
            got(("x", right_unit, k, h), ("xx", right_unit, k, h))
        return jnp.dot(a[left_unit], b[right_unit, k], preferred_element_type=F32)

    def sq(s, k):
        total[0, k] = product(2 * s, 2 * s, k)

    def cra(s, k):
        total[1, k] = product(2 * s + 1, 2 * s, k)

    def crb(s, k):
        total[1, k] += product(2 * s, 2 * s + 1, k)

    def far_names(r):
        return [(kind, r, h) for kind in ("s2", "sf", "sd") for h in (1, 3)]

    def send_far(r):
        p = r % 2
        if r > 1:
            gone(*far_names(r - 2))
        part[p, 1] = total[p, 2].astype(BF)
        send(("s2", r, 1), part.at[p, 1, pl.ds(0, HALF)], far.at[r, 0], at(dz=1))
        send(("s2", r, 3), part.at[p, 1, pl.ds(HALF, HALF)], far.at[r, 1], at(dz=3))

    def free(r, h):
        p, i, k = r % 2, h // 2, h
        where = pl.ds(HALF if h == 1 else 0, HALF)
        part[p, 2 * i, where] = total[p, k, where].astype(BF)
        send(("sf", r, h), part.at[p, 2 * i, where], near.at[r, i, where], at(dz=h))

    def dep(r, h):
        p, i, k = r % 2, h // 2, h
        where = pl.ds(0 if h == 1 else HALF, HALF)
        got(("s2", r, h))
        part[p, 2 * i, where] = (total[p, k, where] + far[r, i].astype(F32)).astype(BF)
        send(("sd", r, h), part.at[p, 2 * i, where], near.at[r, i, where], at(dz=h))

    def keep(which, i, j):
        big_row, big_col = row * (TR // BLK) + i, col * (TC // BLK) + j
        return jnp.where(big_row == big_col, 1, patterns[which, big_row, big_col]).astype(F32)

    inv_root = 1.0 / math.sqrt(6144)

    def finish(r):
        p = r % 2
        got(("sf", r, 1), ("sf", r, 3), ("sd", r, 1), ("sd", r, 3))

        @pl.loop(0, TR // BLK)
        def _(i):
            where = pl.ds(pl.multiple_of(i * BLK, BLK), BLK)
            for j in range(TC // BLK):
                cs = slice(j * BLK, (j + 1) * BLK)
                mine = pl.ds(pl.multiple_of(y * TC + j * BLK, BLK), BLK)
                value = (
                    total[p, 0, where, cs]
                    + near[r, 0, where, cs].astype(F32)
                    + near[r, 1, where, cs].astype(F32)
                ) * inv_root
                if r < 2:
                    a[r + 2, where, mine] = (keep(p, i, j) * value).astype(BF)
                else:
                    value = 2.0 * a[r, where, mine].astype(F32) - value
                    out = (out_zero, out_first)[p]
                    out[where, cs] = keep(p, i, j) * value

    def iota(shape, dim):
        return lax.broadcasted_iota(I32, shape, dim)

    def ones(condition):
        return jnp.where(condition, 1.0, 0.0).astype(BF)

    def strips_place():
        named = jnp.broadcast_to(dest[...].astype(F32), (ITEMS, ITEMS))
        square = (ITEMS, ITEMS)
        earlier = (named == named.T) & (iota(square, 1) < iota(square, 0))
        rank = jnp.sum(jnp.where(earlier, 1.0, 0.0), axis=1, keepdims=True).astype(I32)
        d = dest[...]
        place = (d & 3) * 64 + (d >> 4) * 8 + ((d >> 2) & 3) * 2 + rank
        atom = jnp.broadcast_to(atoms[...].astype(F32), square).T
        block = jnp.broadcast_to(blocks[...].astype(F32), square).T
        lane = iota(square, 1)
        tags = jnp.where(lane == 0, atom + 1.0, jnp.where(lane == 1, block, 0.0))
        rows[:, : ATOM * BLK] = strips[...]
        rows[:, ATOM * BLK :] = tags.astype(BF)
        spread = ones(iota((ITEMS, SLOTS), 1) == place)
        sent[0] = lax.dot_general(
            spread, rows[...], (((0,), (0,)), ((), ())), preferred_element_type=F32
        ).astype(BF)

    def reorder(i, source):
        taken = ones(iota((SLOTS, SLOTS), 1) == source(iota((SLOTS, SLOTS), 0)))
        sent[i] = jnp.dot(taken, came[i - 1], preferred_element_type=F32).astype(BF)

    def strips_y():
        src = rows_at(y, 64)
        for dy in (2, 1, 3):
            send(("gy", dy), sent.at[0, rows_at(lax.rem(y + dy, 4), 64)], came.at[0, src], at(dy=dy))
        move(("gy", 0), sent.at[0, src], came.at[0, src])

    def strips_x():
        got(("gy", 0), ("gy", 1), ("gy", 2), ("gy", 3))
        reorder(1, lambda o: ((o >> 1) & 3) * 64 + (o >> 5) * 8 + ((o >> 3) & 3) * 2 + (o & 1))
        mine = rows_at(row, 32)
        for dx in (2, 1, 3, 0):
            for dc in (0, 1):
                if dx or dc:
                    target = lax.rem(x + dx, 4) * 2 + lax.rem(core + dc, 2)
                    src = sent.at[1, rows_at(target, 32)]
                    send(("gx", dx, dc), src, came.at[1, mine], at(dx=dx, dc=dc))
        move(("gx", 0, 0), sent.at[1, mine], came.at[1, mine])

    def strips_z():
        got(*(("gx", dx, dc) for dx in range(4) for dc in range(2)))
        reorder(2, lambda o: ((o >> 3) & 7) * 32 + (o >> 6) * 8 + (o & 7))
        mine = rows_at(z, 64)
        for dz in (2, 1, 3):
            send(("gz", dz), sent.at[2, rows_at(lax.rem(z + dz, 4), 64)], came.at[2, mine], at(dz=dz))
        move(("gz", 0), sent.at[2, mine], came.at[2, mine])

    def field():
        got(("gz", 0), ("gz", 1), ("gz", 2), ("gz", 3))
        tags = came[2, :, ATOM * BLK :].astype(F32)
        atom, block = tags[:, 0:1], tags[:, 1:2]
        cell = jnp.where(atom > 0.0, block * ATOMS + atom - 1.0, -1.0)
        placing = ones(iota((SLOTS, TC), 1).astype(F32) == cell)
        summed = lax.dot_general(
            placing, came[2, :, : ATOM * BLK], (((0,), (0,)), ((), ())), preferred_element_type=F32
        )
        for j in range(TC // BLK):
            for i in range(ATOM):
                placed[j, pl.ds(i, ATOMS, stride=ATOM), :] = summed[
                    j * ATOMS : (j + 1) * ATOMS, i * BLK : (i + 1) * BLK
                ]

        @pl.loop(0, TR // BLK)
        def _(i):
            where = pl.ds(pl.multiple_of(i * BLK, BLK), BLK)
            for j in range(TC // BLK):
                mine = pl.ds(pl.multiple_of(y * TC + j * BLK, BLK), BLK)
                value = keep(2, i, j) * placed[j, where, :]
                a[1, where, mine] = (-value).astype(BF)

    move("zero", zero_hbm, tile(0))
    peers = [at(dx=dx, dc=dc) for dx in range(4) for dc in range(2) if dx or dc]
    peers += [at(dz=d) for d in (1, 2, 3)] + [at(dy=d) for d in (1, 2, 3)]
    barrier = pltpu.get_barrier_semaphore()
    for peer in peers:
        pl.semaphore_signal(barrier, inc=1, device_id=peer, device_id_type=MESH)
    strips_place()
    pl.semaphore_wait(barrier, len(peers))

    strips_y()
    begin_turn(0)
    begin_side(0)
    strips_x()
    turn_z(0)
    own(0, 2)
    strips_z()
    fwd(0, 2, 3)
    fwd(0, 2, 1)
    side_on(0, 1)
    own(0, 1)
    own(0, 3)
    side_on(0, 3)
    last(0, 2, 3)
    last(0, 2, 1)
    field()
    begin_turn(1)
    begin_side(1)
    fwd(0, 1, 3)
    fwd(0, 1, 1)
    own(0, 0)
    sq(0, 2)
    send_far(0)
    fwd(0, 3, 1)
    fwd(0, 3, 3)
    turn_z(1)
    last(0, 1, 3)
    last(0, 1, 1)
    sq(0, 1)
    free(0, 1)
    fwd(0, 0, 3)
    dep(0, 1)
    fwd(0, 0, 1)
    own(1, 2)
    last(0, 3, 3)
    side_on(1, 3)
    last(0, 3, 1)
    side_on(1, 1)
    last(0, 0, 3)
    last(0, 0, 1)
    sq(0, 3)
    free(0, 3)
    own(1, 1)
    dep(0, 3)
    sq(0, 0)
    fwd(1, 2, 1)
    fwd(1, 2, 3)
    own(1, 3)
    cra(0, 2)
    fwd(1, 1, 1)
    fwd(1, 1, 3)
    own(1, 0)
    last(1, 2, 3)
    last(1, 2, 1)
    cra(0, 1)
    cra(0, 0)
    crb(0, 2)
    fwd(1, 3, 1)
    send_far(1)
    last(1, 1, 1)
    fwd(1, 3, 3)
    last(1, 1, 3)
    cra(0, 3)
    crb(0, 1)
    finish(0)
    begin_turn(2)
    begin_side(2)
    last(1, 3, 3)
    fwd(1, 0, 3)
    last(1, 3, 1)
    fwd(1, 0, 1)
    free(1, 1)
    dep(1, 1)
    crb(0, 3)
    free(1, 3)
    turn_z(2)
    last(1, 0, 1)
    last(1, 0, 3)
    crb(0, 0)
    dep(1, 3)
    side_on(2, 3)
    side_on(2, 1)
    own(2, 2)
    own(2, 1)
    fwd(2, 2, 3)
    fwd(2, 2, 1)
    own(2, 3)
    finish(1)
    begin_turn(3)
    fwd(2, 1, 1)
    begin_side(3)
    fwd(2, 1, 3)
    last(2, 2, 3)
    last(2, 2, 1)
    sq(1, 2)
    send_far(2)
    fwd(2, 3, 3)
    fwd(2, 3, 1)
    turn_z(3)
    last(2, 1, 1)
    last(2, 1, 3)
    last(2, 3, 3)
    last(2, 3, 1)
    side_on(3, 1)
    side_on(3, 3)
    sq(1, 1)
    own(3, 2)
    free(2, 1)
    dep(2, 1)
    sq(1, 3)
    free(2, 3)
    dep(2, 3)
    own(3, 1)
    fwd(3, 2, 3)
    fwd(3, 2, 1)
    own(3, 3)
    cra(1, 2)
    fwd(3, 1, 1)
    fwd(3, 1, 3)
    cra(1, 1)
    last(3, 2, 1)
    last(3, 2, 3)
    cra(1, 3)
    crb(1, 2)
    send_far(3)
    fwd(3, 3, 1)
    fwd(3, 3, 3)
    own(3, 0)
    last(3, 1, 1)
    last(3, 1, 3)
    last(3, 3, 1)
    last(3, 3, 3)
    crb(1, 1)
    free(3, 1)
    crb(1, 3)
    free(3, 3)
    fwd(3, 0, 3)
    fwd(3, 0, 1)
    dep(3, 1)
    last(3, 0, 3)
    last(3, 0, 1)
    own(2, 0)
    dep(3, 3)
    fwd(2, 0, 3)
    fwd(2, 0, 1)
    last(2, 0, 3)
    last(2, 0, 1)
    cra(1, 0)
    crb(1, 0)
    sq(1, 0)
    finish(2)
    finish(3)

    got(*copies, *moves)
    gone(*copies)


def on_device(density, strips, dest_device, atom_slot, block_slot, patterns):
    out = jax.ShapeDtypeStruct((TR, TC), F32)
    vmem = pl.BlockSpec(memory_space=pltpu.VMEM)
    return tuple(pl.pallas_call(
        kernel,
        out_shape=(out, out),
        in_specs=[
            pl.BlockSpec(memory_space=pl.ANY), vmem, vmem, vmem, vmem,
            pl.BlockSpec(memory_space=pltpu.SMEM),
        ],
        out_specs=(vmem, vmem),
        scratch_shapes=[
            pltpu.VMEM((4, TR, KB), BF),
            pltpu.VMEM((4, 4, KB, TC), BF),
            pltpu.VMEM((4, 4, SUB, TC), BF),
            pltpu.VMEM((2, 4, TR, TC), F32),
            pltpu.VMEM((2, 3, TR, TC), BF),
            pltpu.VMEM((4, 2, TR, TC), BF),
            pltpu.VMEM((4, 2, HALF, TC), BF),
            pltpu.VMEM((ITEMS, WIDE), BF),
            pltpu.VMEM((3, SLOTS, WIDE), BF),
            pltpu.VMEM((3, SLOTS, WIDE), BF),
            pltpu.VMEM((TC // BLK, TR, BLK), F32),
            pltpu.SemaphoreType.DMA((N_COPIES,)),
            pltpu.SemaphoreType.DMA((N_COPIES,)),
            pltpu.SemaphoreType.DMA((16,)),
        ],
        compiler_params=pltpu.CompilerParams(
            collective_id=0, has_side_effects=True, vmem_limit_bytes=62 * 2**20 - 2**19
        ),
        cost_estimate=pl.CostEstimate(flops=21743271936, bytes_accessed=8 * 2**20, transcendentals=0),
    )(
        density,
        strips.reshape(ITEMS, ATOM * BLK),
        dest_device,
        atom_slot.reshape(1, ITEMS),
        block_slot.reshape(1, ITEMS),
        patterns,
    ))


def solution(mesh):
    return jax.shard_map(
        on_device,
        mesh=mesh,
        in_specs=(
            P("row", "col"),
            P(("row", "col"), None, None),
            P(("row", "col"), None),
            P(("row", "col")),
            P(("row", "col")),
            P(),
        ),
        out_specs=(P("row", "col"), P("row", "col")),
        check_vma=False,
    )
```

```python
import math

import jax
import jax.numpy as jnp
from jax import lax
from jax.experimental import pallas as pl
from jax.experimental.pallas import tpu as pltpu
from jax.sharding import PartitionSpec as P

MESH = pl.DeviceIdType.MESH
BF = jnp.bfloat16
F32 = jnp.float32
I32 = jnp.int32
TR, TC = 768, 384
HALF = TR // 2
KB = 1536
SUB = TR // 4
BLK = 128
ATOM = 8
ITEMS = 128
SLOTS = 256
WIDE = ATOM * BLK + BLK
ATOMS = TR // ATOM
N_COPIES = 224


def kernel(
    zero_hbm, strips, dest, atoms, blocks, patterns, out_zero, out_first,
    a, b, total, part, near, far, rows, sent, came, placed, send_sem, recv_sem, local_sem,
):
    row, col = lax.axis_index("row"), lax.axis_index("col")
    x, core = row // 2, row % 2
    z, y = col // 4, col % 4

    def at(dx=0, dz=0, dy=0, dc=0):
        nx, nz, ny = (lax.rem(x + dx, 4), lax.rem(z + dz, 4), lax.rem(y + dy, 4))
        return {"row": nx * 2 + lax.rem(core + dc, 2), "col": nz * 4 + ny}

    copies, moves, turns, away = {}, {}, {}, {}
    arrived, left = set(), set()

    def send(name, src, dst, device):
        i = len(copies)
        copies[name] = pltpu.make_async_remote_copy(
            src_ref=src, dst_ref=dst, send_sem=send_sem.at[i], recv_sem=recv_sem.at[i],
            device_id=device, device_id_type=MESH,
        )
        copies[name].start()

    def move(name, src, dst):
        moves[name] = pltpu.make_async_copy(src, dst, local_sem.at[len(moves)])
        moves[name].start()

    def got(*names):
        for name in names:
            if name not in arrived:
                arrived.add(name)
                if name[0] == "t":
                    turns[name].wait_recv()
                elif name in copies:
                    copies[name].wait_recv()
                else:
                    moves[name].wait()

    def gone(*names):
        for name in names:
            if name not in left:
                left.add(name)
                if name[0] == "t" and name[3] == 0:
                    pl.when(away[name])(copies[name].wait_send)
                else:
                    copies[name].wait_send()

    def lanes(position):
        return pl.ds(pl.multiple_of(position * TC, BLK), TC)

    def rows_of(position, first=0, size=SUB):
        return pl.ds(pl.multiple_of(position * TC + core * SUB + first, 32), size)

    def rows_at(position, size):
        return pl.ds(pl.multiple_of(position * size, 16), size)

    def tile(u, where=slice(None)):
        return a.at[u, where, lanes(z)]

    def turn(u):
        if u == 0:
            got(("zero",))
        base = len(copies)
        flip = 1 - lax.rem((lax.rem(y - 2 * core + 4, 4) + 1) // 2, 2)
        for i in range(2):
            h = lax.rem(flip + i, 2)
            quarter = 2 * core + h
            k = lax.rem(y - quarter + 4, 4)
            for e in range(2):
                d = lax.rem(core + e, 2)
                src = tile(u, pl.ds(pl.multiple_of(h * TC + d * SUB, 32), SUB))
                dst = b.at[u, k, pl.ds(pl.multiple_of(x * TC + d * SUB, 32), SUB)]
                name = ("t", u, i, e)
                copies[name] = pltpu.make_async_remote_copy(
                    src_ref=src, dst_ref=dst, send_sem=send_sem.at[base + 2 * i + e],
                    recv_sem=recv_sem.at[base + k],
                    device_id={"row": x * 2 + d, "col": z * 4 + quarter}, device_id_type=MESH,
                )
                if e == 0:
                    away[name] = quarter != y
                    pl.when(quarter != y)(copies[name].start)
                    here = pltpu.make_async_copy(src, dst, recv_sem.at[base + k])
                    pl.when(quarter == y)(here.start)
                else:
                    copies[name].start()
        for k in range(4):
            dst = b.at[u, k, rows_of(x)]
            turns["t", u, k] = pltpu.make_async_remote_copy(
                src_ref=dst, dst_ref=dst, send_sem=send_sem.at[base], recv_sem=recv_sem.at[base + k],
                device_id=at(dc=1), device_id_type=MESH,
            )

    def own(u, k):
        got(("t", u, k))
        src = b.at[u, k, rows_of(x)]
        send(("x", u, k, 1), src, src, at(dx=1))
        send(("x", u, k, 3), src, src, at(dx=3))
        send(("c", u, k, 0), src, src, at(dc=1))

    def fwd(u, k, h):
        got(("x", u, k, h))
        source = lax.rem(x + 4 - h, 4)
        src = b.at[u, k, rows_of(source, SUB // 2 if h == 3 else 0, SUB // 2)]
        send(("xx", u, k, h), src, src, at(dx=h))
        src = b.at[u, k, rows_of(source)]
        send(("c", u, k, h), src, src, at(dc=1))

    def last(u, k, h):
        got(("xx", u, k, h))
        src = b.at[u, k, rows_of(lax.rem(x + 2, 4), SUB // 2 if h == 3 else 0, SUB // 2)]
        send(("c", u, k, h + 1), src, src, at(dc=1))

    def side(u):
        if u == 0:
            got(("zero",))
        send(("z", u, 1), tile(u), tile(u), at(dz=1))
        send(("z", u, 3), tile(u), tile(u), at(dz=3))

    def side_on(u, h):
        got(("z", u, h))
        where = pl.ds(HALF if h == 3 else 0, HALF)
        src = a.at[u, where, lanes(lax.rem(z + 4 - h, 4))]
        send(("zz", u, h), src, src, at(dz=h))

    def product(left_unit, right_unit, k):
        got(("z", left_unit, 1), ("z", left_unit, 3), ("zz", left_unit, 1), ("zz", left_unit, 3))
        got(("t", right_unit, k), *(("c", right_unit, k, i) for i in range(5)))
        for h in (1, 3):
            got(("x", right_unit, k, h), ("xx", right_unit, k, h))
        return jnp.dot(a[left_unit], b[right_unit, k], preferred_element_type=F32)

    def sq(s, k):
        total[0, k] = product(2 * s, 2 * s, k)

    def cra(s, k):
        total[1, k] = product(2 * s + 1, 2 * s, k)

    def crb(s, k):
        total[1, k] += product(2 * s, 2 * s + 1, k)

    def far_names(r):
        return [(kind, r, h) for kind in ("s2", "sf", "sd") for h in (1, 3)]

    def send_far(r):
        p = r % 2
        if r > 1:
            gone(*far_names(r - 2))
        part[p, 1] = total[p, 2].astype(BF)
        send(("s2", r, 1), part.at[p, 1, pl.ds(0, HALF)], far.at[r, 0], at(dy=1))
        send(("s2", r, 3), part.at[p, 1, pl.ds(HALF, HALF)], far.at[r, 1], at(dy=3))

    def free(r, h):
        p, i, k = r % 2, h // 2, h
        where = pl.ds(HALF if h == 1 else 0, HALF)
        part[p, 2 * i, where] = total[p, k, where].astype(BF)
        send(("sf", r, h), part.at[p, 2 * i, where], near.at[r, i, where], at(dy=h))

    def dep(r, h):
        p, i, k = r % 2, h // 2, h
        where = pl.ds(0 if h == 1 else HALF, HALF)
        got(("s2", r, h))
        part[p, 2 * i, where] = (total[p, k, where] + far[r, i].astype(F32)).astype(BF)
        send(("sd", r, h), part.at[p, 2 * i, where], near.at[r, i, where], at(dy=h))

    def keep(which, i, j):
        big_row, big_col = row * (TR // BLK) + i, col * (TC // BLK) + j
        return jnp.where(big_row == big_col, 1, patterns[which, big_row, big_col]).astype(F32)

    inv_root = 1.0 / math.sqrt(6144)

    def finish(r):
        p = r % 2
        got(("sf", r, 1), ("sf", r, 3), ("sd", r, 1), ("sd", r, 3))

        @pl.loop(0, TR // BLK)
        def _(i):
            where = pl.ds(pl.multiple_of(i * BLK, BLK), BLK)
            for j in range(TC // BLK):
                cs = slice(j * BLK, (j + 1) * BLK)
                mine = pl.ds(pl.multiple_of(z * TC + j * BLK, BLK), BLK)
                value = (
                    total[p, 0, where, cs]
                    + near[r, 0, where, cs].astype(F32)
                    + near[r, 1, where, cs].astype(F32)
                ) * inv_root
                if r < 2:
                    a[r + 2, where, mine] = (keep(p, i, j) * value).astype(BF)
                else:
                    value = 2.0 * a[r, where, mine].astype(F32) - value
                    out = (out_zero, out_first)[p]
                    out[where, cs] = keep(p, i, j) * value

    def iota(shape, dim):
        return lax.broadcasted_iota(I32, shape, dim)

    def ones(condition):
        return jnp.where(condition, 1.0, 0.0).astype(BF)

    def strips_place():
        named = jnp.broadcast_to(dest[...].astype(F32), (ITEMS, ITEMS))
        square = (ITEMS, ITEMS)
        earlier = (named == named.T) & (iota(square, 1) < iota(square, 0))
        rank = jnp.sum(jnp.where(earlier, 1.0, 0.0), axis=1, keepdims=True).astype(I32)
        d = dest[...]
        place = d * 2 + rank
        atom = jnp.broadcast_to(atoms[...].astype(F32), square).T
        block = jnp.broadcast_to(blocks[...].astype(F32), square).T
        lane = iota(square, 1)
        tags = jnp.where(lane == 0, atom + 1.0, jnp.where(lane == 1, block, 0.0))
        rows[:, : ATOM * BLK] = strips[...]
        rows[:, ATOM * BLK :] = tags.astype(BF)
        spread = ones(iota((ITEMS, SLOTS), 1) == place)
        sent[0] = lax.dot_general(
            spread, rows[...], (((0,), (0,)), ((), ())), preferred_element_type=F32
        ).astype(BF)

    def strips_x():
        mine = rows_at(row, 32)
        for dx in (2, 1, 3, 0):
            for dc in (0, 1):
                if dx or dc:
                    target = lax.rem(x + dx, 4) * 2 + lax.rem(core + dc, 2)
                    src = sent.at[0, rows_at(target, 32)]
                    send(("gx", dx, dc), src, came.at[0, mine], at(dx=dx, dc=dc))
        move(("gx", 0, 0), sent.at[0, mine], came.at[0, mine])

    def strips_col():
        got(*(("gx", dx, dc) for dx in range(4) for dc in range(2)))
        o = iota((SLOTS, SLOTS), 0)
        source = ((o >> 1) & 7) * 32 + (o >> 4) * 2 + (o & 1)
        taken = ones(iota((SLOTS, SLOTS), 1) == source)
        sent[1] = jnp.dot(taken, came[0], preferred_element_type=F32).astype(BF)
        mine = rows_at(col, 16)
        for dz in (2, 1, 3, 0):
            for dy in (2, 1, 3, 0):
                if dz or dy:
                    target = lax.rem(z + dz, 4) * 4 + lax.rem(y + dy, 4)
                    src = sent.at[1, rows_at(target, 16)]
                    send(("gc", dz, dy), src, came.at[1, mine], at(dz=dz, dy=dy))
        move(("gc", 0, 0), sent.at[1, mine], came.at[1, mine])

    def field():
        got(*(("gc", dz, dy) for dz in range(4) for dy in range(4)))
        tags = came[1, :, ATOM * BLK :].astype(F32)
        atom, block = tags[:, 0:1], tags[:, 1:2]
        cell = jnp.where(atom > 0.0, block * ATOMS + atom - 1.0, -1.0)
        placing = ones(iota((SLOTS, TC), 1).astype(F32) == cell)
        summed = lax.dot_general(
            placing, came[1, :, : ATOM * BLK], (((0,), (0,)), ((), ())), preferred_element_type=F32
        )
        for j in range(TC // BLK):
            for i in range(ATOM):
                placed[j, pl.ds(i, ATOMS, stride=ATOM), :] = summed[
                    j * ATOMS : (j + 1) * ATOMS, i * BLK : (i + 1) * BLK
                ]

        @pl.loop(0, TR // BLK)
        def _(i):
            where = pl.ds(pl.multiple_of(i * BLK, BLK), BLK)
            for j in range(TC // BLK):
                mine = pl.ds(pl.multiple_of(z * TC + j * BLK, BLK), BLK)
                value = keep(2, i, j) * placed[j, where, :]
                a[1, where, mine] = (-value).astype(BF)

    move(("zero",), zero_hbm, tile(0))
    peers = [at(dx=dx, dc=dc) for dx in range(4) for dc in range(2) if dx or dc]
    peers += [at(dz=dz, dy=dy) for dz in range(4) for dy in range(4) if dz or dy]
    peers += [at(dy=dy, dc=1) for dy in (1, 2, 3)]
    barrier = pltpu.get_barrier_semaphore()
    for peer in peers:
        pl.semaphore_signal(barrier, inc=1, device_id=peer, device_id_type=MESH)
    strips_place()
    pl.semaphore_wait(barrier, len(peers))

    side(0)
    strips_x()
    turn(0)
    own(0, 2)
    own(0, 3)
    strips_col()
    fwd(0, 2, 1)
    own(0, 1)
    side_on(0, 3)
    side_on(0, 1)
    fwd(0, 2, 3)
    fwd(0, 3, 3)
    fwd(0, 1, 3)
    last(0, 2, 1)
    fwd(0, 3, 1)
    own(0, 0)
    last(0, 2, 3)
    field()
    fwd(0, 1, 1)
    side(1)
    fwd(0, 0, 1)
    turn(1)
    fwd(0, 0, 3)
    own(1, 0)
    last(0, 3, 3)
    sq(0, 2)
    send_far(0)
    last(0, 3, 1)
    last(0, 0, 1)
    own(1, 2)
    fwd(1, 0, 3)
    own(1, 3)
    last(0, 1, 3)
    sq(0, 3)
    last(0, 1, 1)
    fwd(1, 2, 1)
    last(0, 0, 3)
    free(0, 3)
    fwd(1, 2, 3)
    sq(0, 1)
    free(0, 1)
    fwd(1, 3, 1)
    side_on(1, 1)
    side_on(1, 3)
    fwd(1, 0, 1)
    own(1, 1)
    last(1, 2, 1)
    last(1, 2, 3)
    dep(0, 1)
    dep(0, 3)
    last(1, 3, 1)
    sq(0, 0)
    fwd(1, 1, 3)
    fwd(1, 3, 3)
    fwd(1, 1, 1)
    cra(0, 2)
    crb(0, 2)
    send_far(1)
    last(1, 1, 3)
    finish(0)
    side(2)
    last(1, 3, 3)
    cra(0, 3)
    turn(2)
    cra(0, 1)
    crb(0, 3)
    last(1, 0, 1)
    free(1, 3)
    last(1, 1, 1)
    crb(0, 1)
    last(1, 0, 3)
    own(2, 2)
    dep(1, 1)
    own(2, 3)
    free(1, 1)
    dep(1, 3)
    own(2, 1)
    fwd(2, 3, 1)
    side_on(2, 3)
    cra(0, 0)
    fwd(2, 2, 1)
    side_on(2, 1)
    fwd(2, 3, 3)
    crb(0, 0)
    own(2, 0)
    fwd(2, 1, 1)
    fwd(2, 2, 3)
    fwd(2, 1, 3)
    last(2, 2, 1)
    last(2, 3, 1)
    finish(1)
    side(3)
    turn(3)
    last(2, 2, 3)
    fwd(2, 0, 3)
    last(2, 1, 1)
    fwd(2, 0, 1)
    sq(1, 2)
    own(3, 2)
    last(2, 0, 3)
    send_far(2)
    last(2, 3, 3)
    last(2, 1, 3)
    own(3, 1)
    own(3, 3)
    sq(1, 3)
    sq(1, 1)
    free(2, 1)
    fwd(3, 2, 3)
    last(2, 0, 1)
    free(2, 3)
    side_on(3, 1)
    side_on(3, 3)
    fwd(3, 2, 1)
    fwd(3, 1, 1)
    dep(2, 3)
    fwd(3, 3, 3)
    dep(2, 1)
    fwd(3, 1, 3)
    last(3, 2, 3)
    fwd(3, 3, 1)
    sq(1, 0)
    last(3, 3, 3)
    own(3, 0)
    last(3, 1, 1)
    last(3, 3, 1)
    last(3, 1, 3)
    last(3, 2, 1)
    cra(1, 2)
    crb(1, 2)
    send_far(3)
    cra(1, 3)
    crb(1, 3)
    free(3, 3)
    cra(1, 1)
    crb(1, 1)
    free(3, 1)
    cra(1, 0)
    fwd(3, 0, 3)
    dep(3, 3)
    dep(3, 1)
    fwd(3, 0, 1)
    last(3, 0, 3)
    last(3, 0, 1)
    crb(1, 0)
    finish(2)
    finish(3)

    gone(*copies)


def on_device(density, strips, dest_device, atom_slot, block_slot, patterns):
    out = jax.ShapeDtypeStruct((TR, TC), F32)
    vmem = pl.BlockSpec(memory_space=pltpu.VMEM)
    return tuple(pl.pallas_call(
        kernel,
        out_shape=(out, out),
        in_specs=[
            pl.BlockSpec(memory_space=pl.ANY), vmem, vmem, vmem, vmem,
            pl.BlockSpec(memory_space=pltpu.SMEM),
        ],
        out_specs=(vmem, vmem),
        scratch_shapes=[
            pltpu.VMEM((4, TR, KB), BF),
            pltpu.VMEM((4, 4, KB, TC), BF),
            pltpu.VMEM((2, 4, TR, TC), F32),
            pltpu.VMEM((2, 3, TR, TC), BF),
            pltpu.VMEM((4, 2, TR, TC), BF),
            pltpu.VMEM((4, 2, HALF, TC), BF),
            pltpu.VMEM((ITEMS, WIDE), BF),
            pltpu.VMEM((2, SLOTS, WIDE), BF),
            pltpu.VMEM((2, SLOTS, WIDE), BF),
            pltpu.VMEM((TC // BLK, TR, BLK), F32),
            pltpu.SemaphoreType.DMA((N_COPIES,)),
            pltpu.SemaphoreType.DMA((N_COPIES,)),
            pltpu.SemaphoreType.DMA((16,)),
        ],
        compiler_params=pltpu.CompilerParams(
            collective_id=0, has_side_effects=True, vmem_limit_bytes=62 * 2**20 - 2**19
        ),
        cost_estimate=pl.CostEstimate(flops=21743271936, bytes_accessed=8 * 2**20, transcendentals=0),
    )(
        density,
        strips.reshape(ITEMS, ATOM * BLK),
        dest_device,
        atom_slot.reshape(1, ITEMS),
        block_slot.reshape(1, ITEMS),
        patterns,
    ))


def solution(mesh):
    return jax.shard_map(
        on_device,
        mesh=mesh,
        in_specs=(
            P("row", "col"),
            P(("row", "col"), None, None),
            P(("row", "col"), None),
            P(("row", "col")),
            P(("row", "col")),
            P(),
        ),
        out_specs=(P("row", "col"), P("row", "col")),
        check_vma=False,
    )
```

```python
import math

import jax
import jax.numpy as jnp
from jax import lax
from jax.experimental import pallas as pl
from jax.experimental.pallas import tpu as pltpu
from jax.sharding import PartitionSpec as P

MESH = pl.DeviceIdType.MESH
BF = jnp.bfloat16
F32 = jnp.float32
I32 = jnp.int32
TR, TC = 768, 384
HALF = TR // 2
KB = 1536
SUB = TR // 4
BLK = 128
ATOM = 8
ITEMS = 128
SLOTS = 256
WIDE = ATOM * BLK + BLK
ATOMS = TR // ATOM
N_COPIES = 256


def kernel(
    zero_hbm, strips_hbm, dest, atoms, blocks, patterns_hbm, out_zero, out_first,
    a, b, total, part, near, far, rows, sent, came, placed, strips, patterns, send_sem, recv_sem, local_sem,
):
    row, col = lax.axis_index("row"), lax.axis_index("col")
    x, core = row // 2, row % 2
    z, y = col // 4, col % 4

    def at(dx=0, dz=0, dy=0, dc=0):
        nx, nz, ny = (lax.rem(x + dx, 4), lax.rem(z + dz, 4), lax.rem(y + dy, 4))
        return {"row": nx * 2 + lax.rem(core + dc, 2), "col": nz * 4 + ny}

    copies, moves, turns, bases, away = {}, {}, {}, {}, {}
    arrived, left = set(), set()
    used = [0]

    def take(n):
        used[0] += n
        return used[0] - n

    def send(name, src, dst, device):
        i = take(1)
        copies[name] = pltpu.make_async_remote_copy(
            src_ref=src, dst_ref=dst, send_sem=send_sem.at[i], recv_sem=recv_sem.at[i],
            device_id=device, device_id_type=MESH,
        )
        copies[name].start()

    def move(name, src, dst):
        moves[name] = pltpu.make_async_copy(src, dst, local_sem.at[len(moves)])
        moves[name].start()

    def got(*names):
        for name in names:
            if name not in arrived:
                arrived.add(name)
                if name[0] == "t":
                    turns[name].wait_recv()
                elif name in copies:
                    copies[name].wait_recv()
                else:
                    moves[name].wait()

    def gone(*names):
        for name in names:
            if name not in left:
                left.add(name)
                if name[0] == "t" and name[3] == 0:
                    pl.when(away[name])(copies[name].wait_send)
                else:
                    copies[name].wait_send()

    def lanes(position):
        return pl.ds(pl.multiple_of(position * TC, BLK), TC)

    def rows_of(position, first=0, size=SUB):
        return pl.ds(pl.multiple_of(position * TC + core * SUB + first, 32), size)

    def rows_at(position, size):
        return pl.ds(pl.multiple_of(position * size, 16), size)

    def tile(u, where=slice(None)):
        return a.at[u, where, lanes(z)]

    def turn(u, hh):
        if u == 0:
            got(("zero",))
        if ("t", u, 0) not in turns:
            base = take(4)
            for k in range(4):
                dst = b.at[u, k, rows_of(x)]
                turns["t", u, k] = pltpu.make_async_remote_copy(
                    src_ref=dst, dst_ref=dst, send_sem=send_sem.at[base],
                    recv_sem=recv_sem.at[base + k], device_id=at(dc=1), device_id_type=MESH,
                )
            bases[u] = base
        base = bases[u]
        quarter = 2 * core + hh
        k = lax.rem(y - quarter + 4, 4)
        for e in (1, 0):
            d = lax.rem(core + e, 2)
            src = tile(u, pl.ds(pl.multiple_of(hh * TC + d * SUB, 32), SUB))
            dst = b.at[u, k, pl.ds(pl.multiple_of(x * TC + d * SUB, 32), SUB)]
            name = ("t", u, hh, e)
            copies[name] = pltpu.make_async_remote_copy(
                src_ref=src, dst_ref=dst, send_sem=send_sem.at[base + 2 * hh + e],
                recv_sem=recv_sem.at[base + k],
                device_id={"row": x * 2 + d, "col": z * 4 + quarter}, device_id_type=MESH,
            )
            if e == 0:
                away[name] = quarter != y
                pl.when(quarter != y)(copies[name].start)
                here = pltpu.make_async_copy(src, dst, recv_sem.at[base + k])
                pl.when(quarter == y)(here.start)
            else:
                copies[name].start()

    def own(u, k):
        got(("t", u, k))
        src = b.at[u, k, rows_of(x)]
        send(("x", u, k, 1), src, src, at(dx=1))
        send(("x", u, k, 3), src, src, at(dx=3))
        send(("c", u, k, 0), src, src, at(dc=1))

    def fwd(u, k, h):
        got(("x", u, k, h))
        source = lax.rem(x + 4 - h, 4)
        src = b.at[u, k, rows_of(source, SUB // 2 if h == 3 else 0, SUB // 2)]
        send(("xx", u, k, h), src, src, at(dx=h))
        src = b.at[u, k, rows_of(source)]
        send(("c", u, k, h), src, src, at(dc=1))

    def last(u, k, h):
        got(("xx", u, k, h))
        src = b.at[u, k, rows_of(lax.rem(x + 2, 4), SUB // 2 if h == 3 else 0, SUB // 2)]
        send(("c", u, k, h + 1), src, src, at(dc=1))

    def side(u, hh):
        if u == 0:
            got(("zero",))
        src = tile(u, pl.ds(hh * HALF, HALF))
        send(("z", u, hh, 1), src, src, at(dz=1))
        send(("z", u, hh, 3), src, src, at(dz=3))

    def side_on(u, hh, h):
        got(("z", u, hh, h))
        where = pl.ds(hh * HALF + (SUB if h == 3 else 0), SUB)
        src = a.at[u, where, lanes(lax.rem(z + 4 - h, 4))]
        send(("zz", u, hh, h), src, src, at(dz=h))

    def half_rows(hh):
        return pl.ds(hh * HALF, HALF)

    def product(left_unit, right_unit, k, hh):
        for h in (1, 3):
            got(("z", left_unit, hh, h), ("zz", left_unit, hh, h))
            got(("x", right_unit, k, h), ("xx", right_unit, k, h))
        got(("t", right_unit, k), *(("c", right_unit, k, i) for i in range(5)))
        return jnp.dot(a[left_unit, half_rows(hh)], b[right_unit, k], preferred_element_type=F32)

    def sq(s, k, hh):
        total[0, k, half_rows(hh)] = product(2 * s, 2 * s, k, hh)

    def cra(s, k, hh):
        total[1, k, half_rows(hh)] = product(2 * s + 1, 2 * s, k, hh)

    def crb(s, k, hh):
        total[1, k, half_rows(hh)] += product(2 * s, 2 * s + 1, k, hh)

    def reuse(kind, r, h):
        if r > 1:
            gone((kind, r - 2, h))

    def send_far(r, hh):
        p, h, where = r % 2, 2 * hh + 1, half_rows(hh)
        reuse("s2", r, h)
        part[p, 1, where] = total[p, 2, where].astype(BF)
        send(("s2", r, h), part.at[p, 1, where], far.at[r, hh], at(dy=h))

    def free(r, h):
        p, i, where = r % 2, h // 2, half_rows(1 - h // 2)
        reuse("sf", r, h)
        part[p, 2 * i, where] = total[p, h, where].astype(BF)
        send(("sf", r, h), part.at[p, 2 * i, where], near.at[r, i, where], at(dy=h))

    def dep(r, h):
        p, i, where = r % 2, h // 2, half_rows(h // 2)
        reuse("sd", r, h)
        got(("s2", r, h))
        part[p, 2 * i, where] = (total[p, h, where] + far[r, i].astype(F32)).astype(BF)
        send(("sd", r, h), part.at[p, 2 * i, where], near.at[r, i, where], at(dy=h))

    def keep(which, i, j):
        big_row, big_col = row * (TR // BLK) + i, col * (TC // BLK) + j
        return jnp.where(big_row == big_col, 1, patterns[which, big_row, big_col]).astype(F32)

    inv_root = 1.0 / math.sqrt(6144)

    def finish(r, hh):
        got(("patterns",))
        p = r % 2
        got(("sd" if hh == 0 else "sf", r, 1), ("sf" if hh == 0 else "sd", r, 3))

        @pl.loop(hh * (HALF // BLK), (hh + 1) * (HALF // BLK))
        def _(i):
            where = pl.ds(pl.multiple_of(i * BLK, BLK), BLK)
            for j in range(TC // BLK):
                cs = slice(j * BLK, (j + 1) * BLK)
                mine = pl.ds(pl.multiple_of(z * TC + j * BLK, BLK), BLK)
                value = (
                    total[p, 0, where, cs]
                    + near[r, 0, where, cs].astype(F32)
                    + near[r, 1, where, cs].astype(F32)
                ) * inv_root
                if r < 2:
                    a[r + 2, where, mine] = (keep(p, i, j) * value).astype(BF)
                else:
                    value = 2.0 * a[r, where, mine].astype(F32) - value
                    out = (out_zero, out_first)[p]
                    out[where, cs] = keep(p, i, j) * value

    def iota(shape, dim):
        return lax.broadcasted_iota(I32, shape, dim)

    def ones(condition):
        return jnp.where(condition, 1.0, 0.0).astype(BF)

    def strips_place():
        square = (ITEMS, ITEMS)

        def across(ref):
            return jnp.broadcast_to(ref[...].astype(F32), square)

        named, own_name = across(dest), across(dest).T
        earlier = (named == own_name) & (iota(square, 1) < iota(square, 0))
        rank = jnp.sum(jnp.where(earlier, 1.0, 0.0), axis=1, keepdims=True)
        place = (own_name[:, 0:1] * 2.0 + rank).astype(I32)
        lane = iota(square, 1)
        tags = jnp.where(
            lane == 0, across(atoms).T + 1.0, jnp.where(lane == 1, across(blocks).T, 0.0)
        )
        rows[:, ATOM * BLK :] = tags.astype(BF)
        spread = ones(iota((ITEMS, SLOTS), 1) == place)
        got(("strips",))
        placed[0 : ITEMS * ATOM] = strips[...].astype(F32)
        for i in range(ATOM):
            lines = placed[pl.ds(i, ITEMS, stride=ATOM), :]
            rows[:, i * BLK : (i + 1) * BLK] = lines.astype(BF)
        sent[0] = lax.dot_general(
            spread, rows[...], (((0,), (0,)), ((), ())), preferred_element_type=F32
        ).astype(BF)

    def strips_x():
        mine = rows_at(row, 32)
        for dx in (2, 1, 3, 0):
            for dc in (0, 1):
                if dx or dc:
                    target = lax.rem(x + dx, 4) * 2 + lax.rem(core + dc, 2)
                    src = sent.at[0, rows_at(target, 32)]
                    send(("gx", dx, dc), src, came.at[0, mine], at(dx=dx, dc=dc))
        move(("gx", 0, 0), sent.at[0, mine], came.at[0, mine])

    def strips_col():
        got(*(("gx", dx, dc) for dx in range(4) for dc in range(2)))
        o = iota((SLOTS, SLOTS), 0)
        source = ((o >> 1) & 7) * 32 + (o >> 4) * 2 + (o & 1)
        taken = ones(iota((SLOTS, SLOTS), 1) == source)
        sent[1] = jnp.dot(taken, came[0], preferred_element_type=F32).astype(BF)
        mine = rows_at(col, 16)
        for dz in (2, 1, 3, 0):
            for dy in (2, 1, 3, 0):
                if dz or dy:
                    target = lax.rem(z + dz, 4) * 4 + lax.rem(y + dy, 4)
                    src = sent.at[1, rows_at(target, 16)]
                    send(("gc", dz, dy), src, came.at[1, mine], at(dz=dz, dy=dy))
        move(("gc", 0, 0), sent.at[1, mine], came.at[1, mine])

    def field():
        got(("patterns",))
        got(*(("gc", dz, dy) for dz in range(4) for dy in range(4)))
        tags = came[1, :, ATOM * BLK :].astype(F32)
        atom, block = tags[:, 0:1], tags[:, 1:2]
        cell = jnp.where(atom > 0.0, block * ATOMS + atom - 1.0, -1.0)
        placing = ones(iota((SLOTS, TC), 1).astype(F32) == cell)
        summed = lax.dot_general(
            placing, came[1, :, : ATOM * BLK], (((0,), (0,)), ((), ())), preferred_element_type=F32
        )
        for j in range(TC // BLK):
            for i in range(ATOM):
                placed[pl.ds(j * TR + i, ATOMS, stride=ATOM), :] = summed[
                    j * ATOMS : (j + 1) * ATOMS, i * BLK : (i + 1) * BLK
                ]

        @pl.loop(0, TR // BLK)
        def _(i):
            where = pl.ds(pl.multiple_of(i * BLK, BLK), BLK)
            for j in range(TC // BLK):
                mine = pl.ds(pl.multiple_of(z * TC + j * BLK, BLK), BLK)
                value = keep(2, i, j) * placed[pl.ds(pl.multiple_of(j * TR + i * BLK, BLK), BLK), :]
                a[1, where, mine] = (-value).astype(BF)

    move(("strips",), strips_hbm, strips)
    move(("zero",), zero_hbm, tile(0))
    move(("patterns",), patterns_hbm, patterns)
    peers = [at(dx=dx, dc=dc) for dx in range(4) for dc in range(2) if dx or dc]
    peers += [at(dz=dz, dy=dy) for dz in range(4) for dy in range(4) if dz or dy]
    peers += [at(dy=dy, dc=1) for dy in (1, 2, 3)]
    barrier = pltpu.get_barrier_semaphore()
    for peer in peers:
        pl.semaphore_signal(barrier, inc=1, device_id=peer, device_id_type=MESH)
    strips_place()
    pl.semaphore_wait(barrier, len(peers))

    strips_x()
    turn(0, 1)
    side(0, 0)
    turn(0, 0)
    strips_col()
    own(0, 2)
    own(0, 1)
    side(0, 1)
    own(0, 3)
    fwd(0, 1, 1)
    side_on(0, 0, 1)
    fwd(0, 2, 1)
    fwd(0, 2, 3)
    own(0, 0)
    field()
    turn(1, 0)
    side_on(0, 0, 3)
    side_on(0, 1, 1)
    fwd(0, 1, 3)
    fwd(0, 3, 3)
    turn(1, 1)
    last(0, 2, 1)
    last(0, 2, 3)
    fwd(0, 3, 1)
    side_on(0, 1, 3)
    sq(0, 2, 0)
    fwd(0, 0, 1)
    send_far(0, 0)
    last(0, 1, 1)
    side(1, 0)
    last(0, 1, 3)
    last(0, 3, 3)
    last(0, 3, 1)
    own(1, 2)
    fwd(0, 0, 3)
    sq(0, 2, 1)
    send_far(0, 1)
    sq(0, 1, 1)
    sq(0, 1, 0)
    own(1, 1)
    fwd(1, 2, 1)
    side(1, 1)
    sq(0, 3, 0)
    dep(0, 1)
    free(0, 3)
    own(1, 0)
    sq(0, 3, 1)
    fwd(1, 1, 3)
    last(0, 0, 1)
    fwd(1, 2, 3)
    free(0, 1)
    side_on(1, 0, 3)
    dep(0, 3)
    side_on(1, 0, 1)
    own(1, 3)
    last(0, 0, 3)
    sq(0, 0, 1)
    fwd(1, 1, 1)
    last(1, 2, 1)
    sq(0, 0, 0)
    side_on(1, 1, 1)
    fwd(1, 3, 1)
    last(1, 1, 3)
    cra(0, 3, 0)
    side_on(1, 1, 3)
    fwd(1, 0, 1)
    cra(0, 2, 0)
    fwd(1, 0, 3)
    last(1, 2, 3)
    finish(0, 0)
    turn(2, 0)
    side(2, 0)
    fwd(1, 3, 3)
    last(1, 3, 1)
    crb(0, 2, 0)
    last(1, 1, 1)
    finish(0, 1)
    turn(2, 1)
    send_far(1, 0)
    cra(0, 1, 1)
    last(1, 3, 3)
    cra(0, 2, 1)
    cra(0, 3, 1)
    crb(0, 2, 1)
    last(1, 0, 1)
    send_far(1, 1)
    crb(0, 1, 1)
    own(2, 3)
    own(2, 2)
    cra(0, 1, 0)
    side(2, 1)
    cra(0, 0, 1)
    own(2, 1)
    crb(0, 1, 0)
    crb(0, 3, 0)
    free(1, 3)
    side_on(2, 0, 1)
    dep(1, 1)
    side_on(2, 0, 3)
    fwd(2, 2, 3)
    cra(0, 0, 0)
    fwd(2, 3, 3)
    own(2, 0)
    crb(0, 3, 1)
    fwd(2, 2, 1)
    free(1, 1)
    fwd(2, 3, 1)
    dep(1, 3)
    last(1, 0, 3)
    side_on(2, 1, 3)
    side_on(2, 1, 1)
    crb(0, 0, 1)
    fwd(2, 1, 3)
    fwd(2, 1, 1)
    crb(0, 0, 0)
    finish(1, 0)
    turn(3, 0)
    last(2, 3, 3)
    side(3, 0)
    last(2, 2, 3)
    last(2, 2, 1)
    sq(1, 2, 0)
    sq(1, 2, 1)
    fwd(2, 0, 3)
    last(2, 3, 1)
    last(2, 1, 3)
    last(2, 1, 1)
    finish(1, 1)
    turn(3, 1)
    send_far(2, 0)
    fwd(2, 0, 1)
    side(3, 1)
    sq(1, 1, 1)
    send_far(2, 1)
    own(3, 2)
    free(2, 1)
    side_on(3, 0, 3)
    sq(1, 3, 0)
    own(3, 3)
    side_on(3, 0, 1)
    free(2, 3)
    sq(1, 1, 0)
    sq(1, 3, 1)
    fwd(3, 2, 3)
    side_on(3, 1, 3)
    dep(2, 3)
    fwd(3, 2, 1)
    last(2, 0, 1)
    own(3, 1)
    cra(1, 2, 0)
    side_on(3, 1, 1)
    cra(1, 1, 0)
    dep(2, 1)
    fwd(3, 3, 1)
    cra(1, 3, 0)
    last(3, 2, 1)
    last(3, 2, 3)
    own(3, 0)
    crb(1, 2, 0)
    fwd(3, 3, 3)
    fwd(3, 1, 1)
    cra(1, 2, 1)
    cra(1, 3, 1)
    last(2, 0, 3)
    crb(1, 2, 1)
    send_far(3, 1)
    fwd(3, 1, 3)
    send_far(3, 0)
    last(3, 3, 1)
    cra(1, 1, 1)
    last(3, 3, 3)
    fwd(3, 0, 3)
    crb(1, 3, 0)
    last(3, 1, 1)
    last(3, 1, 3)
    sq(1, 0, 1)
    free(3, 3)
    crb(1, 3, 1)
    crb(1, 1, 1)
    free(3, 1)
    fwd(3, 0, 1)
    crb(1, 1, 0)
    sq(1, 0, 0)
    cra(1, 0, 0)
    finish(2, 1)
    cra(1, 0, 1)
    last(3, 0, 3)
    last(3, 0, 1)
    dep(3, 1)
    dep(3, 3)
    finish(2, 0)
    crb(1, 0, 1)
    crb(1, 0, 0)
    finish(3, 1)
    finish(3, 0)

    gone(*copies)


def hand_on(zero, first, out_zero, out_first, sem):
    copies = []
    for i in range(4):
        where = pl.ds(i * SUB, SUB)
        for src, dst in ((zero, out_zero), (first, out_first)):
            copies.append(pltpu.make_async_copy(src.at[where], dst.at[where], sem.at[len(copies)]))
            copies[-1].start()
    for copy in copies:
        copy.wait()


def on_device(density, strips, dest_device, atom_slot, block_slot, patterns):
    out = jax.ShapeDtypeStruct((TR, TC), F32)
    vmem = pl.BlockSpec(memory_space=pltpu.VMEM)
    hbm = pl.BlockSpec(memory_space=pl.ANY)
    results = pl.pallas_call(
        kernel,
        out_shape=(out, out),
        in_specs=[
            hbm, hbm, vmem, vmem, vmem, hbm,
        ],
        out_specs=(vmem, vmem),
        scratch_shapes=[
            pltpu.VMEM((4, TR, KB), BF),
            pltpu.VMEM((4, 4, KB, TC), BF),
            pltpu.VMEM((2, 4, TR, TC), F32),
            pltpu.VMEM((2, 3, TR, TC), BF),
            pltpu.VMEM((4, 2, TR, TC), BF),
            pltpu.VMEM((4, 2, HALF, TC), BF),
            pltpu.VMEM((ITEMS, WIDE), BF),
            pltpu.VMEM((2, SLOTS, WIDE), BF),
            pltpu.VMEM((2, SLOTS, WIDE), BF),
            pltpu.VMEM((TC // BLK * TR, BLK), F32),
            pltpu.VMEM((ITEMS * ATOM, BLK), BF),
            pltpu.SMEM((3, 48, 48), I32),
            pltpu.SemaphoreType.DMA((N_COPIES,)),
            pltpu.SemaphoreType.DMA((N_COPIES,)),
            pltpu.SemaphoreType.DMA((16,)),
        ],
        compiler_params=pltpu.CompilerParams(
            collective_id=0, has_side_effects=True, vmem_limit_bytes=62 * 2**20 - 2**19
        ),
        cost_estimate=pl.CostEstimate(flops=21743271936, bytes_accessed=8 * 2**20, transcendentals=0),
    )(
        density,
        strips.reshape(ITEMS * ATOM, BLK),
        dest_device.reshape(1, ITEMS),
        atom_slot.reshape(1, ITEMS),
        block_slot.reshape(1, ITEMS),
        patterns,
    )
    return tuple(pl.pallas_call(
        hand_on,
        out_shape=(out, out),
        in_specs=(hbm, hbm),
        out_specs=(hbm, hbm),
        scratch_shapes=[pltpu.SemaphoreType.DMA((8,))],
    )(*results))


def solution(mesh):
    return jax.shard_map(
        on_device,
        mesh=mesh,
        in_specs=(
            P("row", "col"),
            P(("row", "col"), None, None),
            P(("row", "col"), None),
            P(("row", "col")),
            P(("row", "col")),
            P(),
        ),
        out_specs=(P("row", "col"), P("row", "col")),
        check_vma=False,
    )
```

```python
import math

import jax
import jax.numpy as jnp
from jax import lax
from jax.experimental import pallas as pl
from jax.experimental.pallas import tpu as pltpu
from jax.sharding import PartitionSpec as P

MESH = pl.DeviceIdType.MESH
BF = jnp.bfloat16
F32 = jnp.float32
I32 = jnp.int32
TR, TC = 768, 384
HALF = TR // 2
KB = 1536
SUB = TR // 4
BLK = 128
ATOM = 8
ITEMS = 128
SLOTS = 256
WIDE = ATOM * BLK + BLK
ATOMS = TR // ATOM
N_COPIES = 272


def kernel(
    zero_hbm, strips_hbm, dest, atoms, blocks, patterns_hbm, out_zero, out_first,
    a, b, total, part, near, far, rows, sent, came, placed, strips, patterns, out, send_sem, recv_sem, local_sem,
):
    row, col = lax.axis_index("row"), lax.axis_index("col")
    x, core = row // 2, row % 2
    z, y = col // 4, col % 4

    def at(dx=0, dz=0, dy=0, dc=0):
        nx, nz, ny = (lax.rem(x + dx, 4), lax.rem(z + dz, 4), lax.rem(y + dy, 4))
        return {"row": nx * 2 + lax.rem(core + dc, 2), "col": nz * 4 + ny}

    copies, moves, turns, bases, away = {}, {}, {}, {}, {}
    arrived, left = set(), set()
    used = [0]

    def take(n):
        used[0] += n
        return used[0] - n

    def send(name, src, dst, device):
        i = take(1)
        copies[name] = pltpu.make_async_remote_copy(
            src_ref=src, dst_ref=dst, send_sem=send_sem.at[i], recv_sem=recv_sem.at[i],
            device_id=device, device_id_type=MESH,
        )
        copies[name].start()

    def move(name, src, dst):
        moves[name] = pltpu.make_async_copy(src, dst, local_sem.at[len(moves)])
        moves[name].start()

    def got(*names):
        for name in names:
            if name not in arrived:
                arrived.add(name)
                if name[0] == "t":
                    turns[name].wait_recv()
                elif name in copies:
                    copies[name].wait_recv()
                else:
                    moves[name].wait()

    def gone(*names):
        for name in names:
            if name not in left:
                left.add(name)
                if name[0] == "t" and name[3] == 0:
                    pl.when(away[name])(copies[name].wait_send)
                else:
                    copies[name].wait_send()

    def lanes(position):
        return pl.ds(pl.multiple_of(position * TC, BLK), TC)

    def rows_of(position, first=0, size=SUB):
        return pl.ds(pl.multiple_of(position * TC + core * SUB + first, 32), size)

    def rows_at(position, size):
        return pl.ds(pl.multiple_of(position * size, 16), size)

    def tile(u, where=slice(None)):
        return a.at[u, where, lanes(z)]

    def turn(u, hh):
        if u == 0:
            got(("zero",))
        if ("t", u, 0) not in turns:
            base = take(4)
            for k in range(4):
                dst = b.at[u, k, rows_of(x)]
                turns["t", u, k] = pltpu.make_async_remote_copy(
                    src_ref=dst, dst_ref=dst, send_sem=send_sem.at[base],
                    recv_sem=recv_sem.at[base + k], device_id=at(dc=1), device_id_type=MESH,
                )
            bases[u] = base
        base = bases[u]
        quarter = 2 * core + hh
        k = lax.rem(y - quarter + 4, 4)
        for e in (1, 0):
            d = lax.rem(core + e, 2)
            src = tile(u, pl.ds(pl.multiple_of(hh * TC + d * SUB, 32), SUB))
            dst = b.at[u, k, pl.ds(pl.multiple_of(x * TC + d * SUB, 32), SUB)]
            name = ("t", u, hh, e)
            copies[name] = pltpu.make_async_remote_copy(
                src_ref=src, dst_ref=dst, send_sem=send_sem.at[base + 2 * hh + e],
                recv_sem=recv_sem.at[base + k],
                device_id={"row": x * 2 + d, "col": z * 4 + quarter}, device_id_type=MESH,
            )
            if e == 0:
                away[name] = quarter != y
                pl.when(quarter != y)(copies[name].start)
                here = pltpu.make_async_copy(src, dst, recv_sem.at[base + k])
                pl.when(quarter == y)(here.start)
            else:
                copies[name].start()

    def own(u, k):
        got(("t", u, k))
        src = b.at[u, k, rows_of(x)]
        send(("x", u, k, 1), src, src, at(dx=1))
        send(("x", u, k, 3), src, src, at(dx=3))
        send(("c", u, k, 0), src, src, at(dc=1))

    def fwd(u, k, h):
        got(("x", u, k, h))
        source = lax.rem(x + 4 - h, 4)
        src = b.at[u, k, rows_of(source, SUB // 2 if h == 3 else 0, SUB // 2)]
        send(("xx", u, k, h), src, src, at(dx=h))
        src = b.at[u, k, rows_of(source)]
        send(("c", u, k, h), src, src, at(dc=1))

    def last(u, k, h):
        got(("xx", u, k, h))
        src = b.at[u, k, rows_of(lax.rem(x + 2, 4), SUB // 2 if h == 3 else 0, SUB // 2)]
        send(("c", u, k, h + 1), src, src, at(dc=1))

    def side(u, hh):
        if u == 0:
            got(("zero",))
        src = tile(u, pl.ds(hh * HALF, HALF))
        send(("z", u, hh, 1), src, src, at(dz=1))
        send(("z", u, hh, 3), src, src, at(dz=3))

    def side_on(u, hh, h):
        got(("z", u, hh, h))
        where = pl.ds(hh * HALF + (SUB if h == 3 else 0), SUB)
        src = a.at[u, where, lanes(lax.rem(z + 4 - h, 4))]
        send(("zz", u, hh, h), src, src, at(dz=h))

    def half_rows(hh):
        return pl.ds(hh * HALF, HALF)

    def product(left_unit, right_unit, k, hh):
        for h in (1, 3):
            got(("z", left_unit, hh, h), ("zz", left_unit, hh, h))
            got(("x", right_unit, k, h), ("xx", right_unit, k, h))
        got(("t", right_unit, k), *(("c", right_unit, k, i) for i in range(5)))
        return jnp.dot(a[left_unit, half_rows(hh)], b[right_unit, k], preferred_element_type=F32)

    def sq(s, k, hh):
        total[0, k, half_rows(hh)] = product(2 * s, 2 * s, k, hh)

    def cra(s, k, hh):
        total[1, k, half_rows(hh)] = product(2 * s + 1, 2 * s, k, hh)

    def crb(s, k, hh):
        total[1, k, half_rows(hh)] += product(2 * s, 2 * s + 1, k, hh)

    def reuse(kind, r, hh, h):
        if r > 1:
            gone((kind, r - 2, hh, h))

    def send_far(r, hh):
        p, where = r % 2, half_rows(hh)
        for h in (1, 3):
            reuse("s2", r, hh, h)
        part[p, 1, where] = total[p, 2, where].astype(BF)
        for h in (1, 3):
            where = pl.ds(hh * HALF + h // 2 * SUB, SUB)
            send(("s2", r, hh, h), part.at[p, 1, where], far.at[r, where], at(dy=h))

    def free(r, hh, h):
        p, i, where = r % 2, h // 2, pl.ds(hh * HALF + (1 - h // 2) * SUB, SUB)
        reuse("sf", r, hh, h)
        part[p, 2 * i, where] = total[p, h, where].astype(BF)
        send(("sf", r, hh, h), part.at[p, 2 * i, where], near.at[r, i, where], at(dy=h))

    def dep(r, hh, h):
        p, i, where = r % 2, h // 2, pl.ds(hh * HALF + h // 2 * SUB, SUB)
        reuse("sd", r, hh, h)
        got(("s2", r, hh, h))
        part[p, 2 * i, where] = (total[p, h, where] + far[r, where].astype(F32)).astype(BF)
        send(("sd", r, hh, h), part.at[p, 2 * i, where], near.at[r, i, where], at(dy=h))

    def keep(which, i, j):
        big_row, big_col = row * (TR // BLK) + i, col * (TC // BLK) + j
        return jnp.where(big_row == big_col, 1, patterns[which, big_row, big_col]).astype(F32)

    inv_root = 1.0 / math.sqrt(6144)

    def finish(r, hh):
        got(("patterns",))
        p = r % 2
        got(*((kind, r, hh, h) for kind in ("sf", "sd") for h in (1, 3)))

        @pl.loop(hh * (HALF // BLK), (hh + 1) * (HALF // BLK))
        def _(i):
            where = pl.ds(pl.multiple_of(i * BLK, BLK), BLK)
            for j in range(TC // BLK):
                cs = slice(j * BLK, (j + 1) * BLK)
                mine = pl.ds(pl.multiple_of(z * TC + j * BLK, BLK), BLK)
                value = (
                    total[p, 0, where, cs]
                    + near[r, 0, where, cs].astype(F32)
                    + near[r, 1, where, cs].astype(F32)
                ) * inv_root
                if r < 2:
                    a[r + 2, where, mine] = (keep(p, i, j) * value).astype(BF)
                else:
                    value = 2.0 * a[r, where, mine].astype(F32) - value
                    out[p, where, cs] = keep(p, i, j) * value

        if r > 1:
            where = half_rows(hh)
            move(("out", p, hh), out.at[p, where], (out_zero, out_first)[p].at[where])

    def iota(shape, dim):
        return lax.broadcasted_iota(I32, shape, dim)

    def ones(condition):
        return jnp.where(condition, 1.0, 0.0).astype(BF)

    def strips_place():
        square = (ITEMS, ITEMS)

        def across(ref):
            return jnp.broadcast_to(ref[...].astype(F32), square)

        named, own_name = across(dest), across(dest).T
        earlier = (named == own_name) & (iota(square, 1) < iota(square, 0))
        rank = jnp.sum(jnp.where(earlier, 1.0, 0.0), axis=1, keepdims=True)
        place = (own_name[:, 0:1] * 2.0 + rank).astype(I32)
        lane = iota(square, 1)
        tags = jnp.where(
            lane == 0, across(atoms).T + 1.0, jnp.where(lane == 1, across(blocks).T, 0.0)
        )
        rows[:, ATOM * BLK :] = tags.astype(BF)
        spread = ones(iota((ITEMS, SLOTS), 1) == place)
        got(("strips",))
        placed[0 : ITEMS * ATOM] = strips[...].astype(F32)
        for i in range(ATOM):
            lines = placed[pl.ds(i, ITEMS, stride=ATOM), :]
            rows[:, i * BLK : (i + 1) * BLK] = lines.astype(BF)
        sent[0] = lax.dot_general(
            spread, rows[...], (((0,), (0,)), ((), ())), preferred_element_type=F32
        ).astype(BF)

    def strips_x():
        mine = rows_at(row, 32)
        for dx in (2, 1, 3, 0):
            for dc in (0, 1):
                if dx or dc:
                    target = lax.rem(x + dx, 4) * 2 + lax.rem(core + dc, 2)
                    src = sent.at[0, rows_at(target, 32)]
                    send(("gx", dx, dc), src, came.at[0, mine], at(dx=dx, dc=dc))
        move(("gx", 0, 0), sent.at[0, mine], came.at[0, mine])

    def strips_col():
        got(*(("gx", dx, dc) for dx in range(4) for dc in range(2)))
        o = iota((SLOTS, SLOTS), 0)
        source = ((o >> 1) & 7) * 32 + (o >> 4) * 2 + (o & 1)
        taken = ones(iota((SLOTS, SLOTS), 1) == source)
        sent[1] = jnp.dot(taken, came[0], preferred_element_type=F32).astype(BF)
        mine = rows_at(col, 16)
        for dz in (2, 1, 3, 0):
            for dy in (2, 1, 3, 0):
                if dz or dy:
                    target = lax.rem(z + dz, 4) * 4 + lax.rem(y + dy, 4)
                    src = sent.at[1, rows_at(target, 16)]
                    send(("gc", dz, dy), src, came.at[1, mine], at(dz=dz, dy=dy))
        move(("gc", 0, 0), sent.at[1, mine], came.at[1, mine])

    def field():
        got(("patterns",))
        got(*(("gc", dz, dy) for dz in range(4) for dy in range(4)))
        tags = came[1, :, ATOM * BLK :].astype(F32)
        atom, block = tags[:, 0:1], tags[:, 1:2]
        cell = jnp.where(atom > 0.0, block * ATOMS + atom - 1.0, -1.0)
        placing = ones(iota((SLOTS, TC), 1).astype(F32) == cell)
        summed = lax.dot_general(
            placing, came[1, :, : ATOM * BLK], (((0,), (0,)), ((), ())), preferred_element_type=F32
        )
        for j in range(TC // BLK):
            for i in range(ATOM):
                placed[pl.ds(j * TR + i, ATOMS, stride=ATOM), :] = summed[
                    j * ATOMS : (j + 1) * ATOMS, i * BLK : (i + 1) * BLK
                ]

        @pl.loop(0, TR // BLK)
        def _(i):
            where = pl.ds(pl.multiple_of(i * BLK, BLK), BLK)
            for j in range(TC // BLK):
                mine = pl.ds(pl.multiple_of(z * TC + j * BLK, BLK), BLK)
                value = keep(2, i, j) * placed[pl.ds(pl.multiple_of(j * TR + i * BLK, BLK), BLK), :]
                a[1, where, mine] = (-value).astype(BF)

    move(("strips",), strips_hbm, strips)
    move(("zero",), zero_hbm, tile(0))
    move(("patterns",), patterns_hbm, patterns)
    peers = [at(dx=dx, dc=dc) for dx in range(4) for dc in range(2) if dx or dc]
    peers += [at(dz=dz, dy=dy) for dz in range(4) for dy in range(4) if dz or dy]
    peers += [at(dy=dy, dc=1) for dy in (1, 2, 3)]
    barrier = pltpu.get_barrier_semaphore()
    for peer in peers:
        pl.semaphore_signal(barrier, inc=1, device_id=peer, device_id_type=MESH)
    strips_place()
    pl.semaphore_wait(barrier, len(peers))

    strips_x()
    turn(0, 1)
    side(0, 1)
    turn(0, 0)
    strips_col()
    side(0, 0)
    own(0, 3)
    side_on(0, 1, 1)
    own(0, 2)
    side_on(0, 1, 3)
    own(0, 1)
    fwd(0, 3, 3)
    fwd(0, 2, 1)
    fwd(0, 2, 3)
    field()
    own(0, 0)
    turn(1, 0)
    fwd(0, 1, 1)
    last(0, 2, 1)
    last(0, 3, 3)
    side_on(0, 0, 3)
    turn(1, 1)
    fwd(0, 1, 3)
    fwd(0, 3, 1)
    side_on(0, 0, 1)
    last(0, 2, 3)
    fwd(0, 0, 1)
    sq(0, 2, 1)
    send_far(0, 1)
    side(1, 1)
    side(1, 0)
    fwd(0, 0, 3)
    last(0, 1, 3)
    own(1, 2)
    last(0, 3, 1)
    own(1, 1)
    sq(0, 2, 0)
    send_far(0, 0)
    last(0, 1, 1)
    sq(0, 3, 1)
    last(0, 0, 1)
    sq(0, 3, 0)
    sq(0, 1, 0)
    free(0, 0, 3)
    free(0, 0, 1)
    dep(0, 1, 3)
    sq(0, 1, 1)
    own(1, 3)
    last(0, 0, 3)
    free(0, 1, 1)
    dep(0, 0, 1)
    fwd(1, 1, 1)
    fwd(1, 2, 3)
    dep(0, 0, 3)
    fwd(1, 2, 1)
    sq(0, 0, 0)
    free(0, 1, 3)
    side_on(1, 1, 3)
    fwd(1, 1, 3)
    side_on(1, 1, 1)
    own(1, 0)
    dep(0, 1, 1)
    side_on(1, 0, 3)
    last(1, 2, 3)
    last(1, 1, 1)
    fwd(1, 3, 1)
    sq(0, 0, 1)
    side_on(1, 0, 1)
    fwd(1, 3, 3)
    last(1, 2, 1)
    finish(0, 0)
    side(2, 0)
    turn(2, 0)
    cra(0, 2, 1)
    cra(0, 1, 1)
    last(1, 1, 3)
    finish(0, 1)
    side(2, 1)
    turn(2, 1)
    cra(0, 2, 0)
    crb(0, 2, 1)
    crb(0, 2, 0)
    fwd(1, 0, 3)
    fwd(1, 0, 1)
    send_far(1, 1)
    crb(0, 1, 1)
    last(1, 3, 3)
    cra(0, 3, 1)
    last(1, 3, 1)
    own(2, 2)
    send_far(1, 0)
    cra(0, 3, 0)
    cra(0, 1, 0)
    own(2, 3)
    crb(0, 3, 1)
    free(1, 1, 1)
    last(1, 0, 3)
    free(1, 1, 3)
    dep(1, 1, 1)
    fwd(2, 2, 3)
    dep(1, 1, 3)
    crb(0, 3, 0)
    side_on(2, 1, 3)
    side_on(2, 1, 1)
    cra(0, 0, 1)
    fwd(2, 2, 1)
    side_on(2, 0, 1)
    crb(0, 1, 0)
    free(1, 0, 3)
    fwd(2, 3, 3)
    free(1, 0, 1)
    own(2, 1)
    dep(1, 0, 1)
    last(1, 0, 1)
    cra(0, 0, 0)
    fwd(2, 3, 1)
    own(2, 0)
    side_on(2, 0, 3)
    last(2, 2, 1)
    last(2, 2, 3)
    crb(0, 0, 1)
    dep(1, 0, 3)
    finish(1, 1)
    last(2, 3, 3)
    side(3, 1)
    turn(3, 1)
    crb(0, 0, 0)
    last(2, 3, 1)
    fwd(2, 1, 3)
    sq(1, 3, 0)
    finish(1, 0)
    fwd(2, 1, 1)
    turn(3, 0)
    side(3, 0)
    last(2, 1, 3)
    sq(1, 2, 1)
    fwd(2, 0, 1)
    sq(1, 2, 0)
    send_far(2, 1)
    last(2, 1, 1)
    own(3, 2)
    send_far(2, 0)
    sq(1, 1, 1)
    dep(2, 1, 1)
    own(3, 3)
    free(2, 0, 3)
    side_on(3, 0, 1)
    side_on(3, 0, 3)
    sq(1, 3, 1)
    dep(2, 1, 3)
    fwd(3, 2, 1)
    sq(1, 1, 0)
    fwd(3, 2, 3)
    fwd(2, 0, 3)
    free(2, 0, 1)
    own(3, 1)
    side_on(3, 1, 1)
    side_on(3, 1, 3)
    fwd(3, 3, 1)
    dep(2, 0, 1)
    free(2, 1, 3)
    cra(1, 1, 0)
    fwd(3, 3, 3)
    last(3, 2, 3)
    last(2, 0, 3)
    cra(1, 2, 0)
    dep(2, 0, 3)
    last(3, 2, 1)
    free(2, 1, 1)
    fwd(3, 1, 1)
    cra(1, 1, 1)
    cra(1, 3, 0)
    crb(1, 2, 0)
    fwd(3, 1, 3)
    send_far(3, 0)
    cra(1, 2, 1)
    last(3, 3, 3)
    last(2, 0, 1)
    crb(1, 2, 1)
    last(3, 1, 1)
    send_far(3, 1)
    own(3, 0)
    last(3, 3, 1)
    sq(1, 0, 0)
    last(3, 1, 3)
    crb(1, 3, 0)
    crb(1, 1, 1)
    free(3, 1, 1)
    free(3, 0, 3)
    dep(3, 0, 3)
    crb(1, 1, 0)
    fwd(3, 0, 3)
    dep(3, 0, 1)
    cra(1, 0, 0)
    free(3, 0, 1)
    fwd(3, 0, 1)
    cra(1, 3, 1)
    crb(1, 3, 1)
    last(3, 0, 3)
    free(3, 1, 3)
    finish(2, 0)
    cra(1, 0, 1)
    last(3, 0, 1)
    crb(1, 0, 0)
    dep(3, 1, 3)
    dep(3, 1, 1)
    finish(3, 0)
    sq(1, 0, 1)
    finish(2, 1)
    crb(1, 0, 1)
    finish(3, 1)

    got(*(name for name in moves if name[0] == "out"))
    gone(*copies)


def hand_on(zero, first, out_zero, out_first, held, in_sem, out_sem):
    ins, outs = [], []
    for i in range(4):
        where = pl.ds(i * SUB, SUB)
        for p, (src, dst) in enumerate(((zero, out_zero), (first, out_first))):
            n, slot = len(ins), held.at[p, where]
            ins.append(pltpu.make_async_copy(src.at[where], slot, in_sem.at[n]))
            outs.append(pltpu.make_async_copy(slot, dst.at[where], out_sem.at[n]))
            ins[n].start()
    for arrive, leave in zip(ins, outs):
        arrive.wait()
        leave.start()
    for leave in outs:
        leave.wait()


def on_device(density, strips, dest_device, atom_slot, block_slot, patterns):
    out = jax.ShapeDtypeStruct((TR, TC), F32)
    vmem = pl.BlockSpec(memory_space=pltpu.VMEM)
    hbm = pl.BlockSpec(memory_space=pl.ANY)
    results = pl.pallas_call(
        kernel,
        out_shape=(out, out),
        in_specs=[
            hbm, hbm, vmem, vmem, vmem, hbm,
        ],
        out_specs=(hbm, hbm),
        scratch_shapes=[
            pltpu.VMEM((4, TR, KB), BF),
            pltpu.VMEM((4, 4, KB, TC), BF),
            pltpu.VMEM((2, 4, TR, TC), F32),
            pltpu.VMEM((2, 3, TR, TC), BF),
            pltpu.VMEM((4, 2, TR, TC), BF),
            pltpu.VMEM((4, TR, TC), BF),
            pltpu.VMEM((ITEMS, WIDE), BF),
            pltpu.VMEM((2, SLOTS, WIDE), BF),
            pltpu.VMEM((2, SLOTS, WIDE), BF),
            pltpu.VMEM((TC // BLK * TR, BLK), F32),
            pltpu.VMEM((ITEMS * ATOM, BLK), BF),
            pltpu.SMEM((3, 48, 48), I32),
            pltpu.VMEM((2, TR, TC), F32),
            pltpu.SemaphoreType.DMA((N_COPIES,)),
            pltpu.SemaphoreType.DMA((N_COPIES,)),
            pltpu.SemaphoreType.DMA((16,)),
        ],
        compiler_params=pltpu.CompilerParams(
            collective_id=0, has_side_effects=True, vmem_limit_bytes=62 * 2**20 - 2**19
        ),
        cost_estimate=pl.CostEstimate(flops=21743271936, bytes_accessed=8 * 2**20, transcendentals=0),
    )(
        density,
        strips.reshape(ITEMS * ATOM, BLK),
        dest_device.reshape(1, ITEMS),
        atom_slot.reshape(1, ITEMS),
        block_slot.reshape(1, ITEMS),
        patterns,
    )
    return tuple(pl.pallas_call(
        hand_on,
        out_shape=(out, out),
        in_specs=(hbm, hbm),
        out_specs=(hbm, hbm),
        scratch_shapes=[
            pltpu.VMEM((2, TR, TC), F32),
            pltpu.SemaphoreType.DMA((8,)),
            pltpu.SemaphoreType.DMA((8,)),
        ],
    )(*results))


def solution(mesh):
    return jax.shard_map(
        on_device,
        mesh=mesh,
        in_specs=(
            P("row", "col"),
            P(("row", "col"), None, None),
            P(("row", "col"), None),
            P(("row", "col")),
            P(("row", "col")),
            P(),
        ),
        out_specs=(P("row", "col"), P("row", "col")),
        check_vma=False,
    )
```

```python
import math

import jax
import jax.numpy as jnp
from jax import lax
from jax.experimental import pallas as pl
from jax.experimental.pallas import tpu as pltpu
from jax.sharding import PartitionSpec as P

MESH = pl.DeviceIdType.MESH
BF = jnp.bfloat16
F32 = jnp.float32
I32 = jnp.int32
TR, TC = 768, 384
HALF = TR // 2
KB = 1536
SUB = TR // 4
BLK = 128
ATOM = 8
ITEMS = 128
SLOTS = 256
WIDE = ATOM * BLK + BLK
ATOMS = TR // ATOM
N_COPIES = 272


def kernel(
    zero_hbm, strips_hbm, dest, atoms, blocks, patterns_hbm, out_zero, out_first,
    a, b, total, part, near, far, rows, sent, came, placed, strips, patterns, out, send_sem, recv_sem, local_sem,
):
    row, col = lax.axis_index("row"), lax.axis_index("col")
    x, core = row // 2, row % 2
    z, y = col // 4, col % 4

    def at(dx=0, dz=0, dy=0, dc=0):
        nx, nz, ny = (lax.rem(x + dx, 4), lax.rem(z + dz, 4), lax.rem(y + dy, 4))
        return {"row": nx * 2 + lax.rem(core + dc, 2), "col": nz * 4 + ny}

    copies, moves, turns, bases, away = {}, {}, {}, {}, {}
    arrived, left = set(), set()
    used = [0]

    def take(n):
        used[0] += n
        return used[0] - n

    def send(name, src, dst, device):
        i = take(1)
        copies[name] = pltpu.make_async_remote_copy(
            src_ref=src, dst_ref=dst, send_sem=send_sem.at[i], recv_sem=recv_sem.at[i],
            device_id=device, device_id_type=MESH,
        )
        copies[name].start()

    def move(name, src, dst):
        moves[name] = pltpu.make_async_copy(src, dst, local_sem.at[len(moves)])
        moves[name].start()

    def got(*names):
        for name in names:
            if name not in arrived:
                arrived.add(name)
                if name[0] == "t":
                    turns[name].wait_recv()
                elif name in copies:
                    copies[name].wait_recv()
                else:
                    moves[name].wait()

    def gone(*names):
        for name in names:
            if name not in left:
                left.add(name)
                if name[0] == "t" and name[3] == 0:
                    pl.when(away[name])(copies[name].wait_send)
                else:
                    copies[name].wait_send()

    def lanes(position):
        return pl.ds(pl.multiple_of(position * TC, BLK), TC)

    def rows_of(position, first=0, size=SUB):
        return pl.ds(pl.multiple_of(position * TC + core * SUB + first, 32), size)

    def rows_at(position, size):
        return pl.ds(pl.multiple_of(position * size, 16), size)

    def tile(u, where=slice(None)):
        return a.at[u, where, lanes(z)]

    def turn(u, hh):
        if u == 0:
            got(("zero",))
        if ("t", u, 0) not in turns:
            base = take(4)
            for k in range(4):
                dst = b.at[u, k, rows_of(x)]
                turns["t", u, k] = pltpu.make_async_remote_copy(
                    src_ref=dst, dst_ref=dst, send_sem=send_sem.at[base],
                    recv_sem=recv_sem.at[base + k], device_id=at(dc=1), device_id_type=MESH,
                )
            bases[u] = base
        base = bases[u]
        quarter = 2 * core + hh
        k = lax.rem(y - quarter + 4, 4)
        for e in (1, 0):
            d = lax.rem(core + e, 2)
            src = tile(u, pl.ds(pl.multiple_of(hh * TC + d * SUB, 32), SUB))
            dst = b.at[u, k, pl.ds(pl.multiple_of(x * TC + d * SUB, 32), SUB)]
            name = ("t", u, hh, e)
            copies[name] = pltpu.make_async_remote_copy(
                src_ref=src, dst_ref=dst, send_sem=send_sem.at[base + 2 * hh + e],
                recv_sem=recv_sem.at[base + k],
                device_id={"row": x * 2 + d, "col": z * 4 + quarter}, device_id_type=MESH,
            )
            if e == 0:
                away[name] = quarter != y
                pl.when(quarter != y)(copies[name].start)
                here = pltpu.make_async_copy(src, dst, recv_sem.at[base + k])
                pl.when(quarter == y)(here.start)
            else:
                copies[name].start()

    def own(u, k):
        got(("t", u, k))
        src = b.at[u, k, rows_of(x)]
        send(("x", u, k, 1), src, src, at(dx=1))
        send(("x", u, k, 3), src, src, at(dx=3))
        send(("c", u, k, 0), src, src, at(dc=1))

    def fwd(u, k, h):
        got(("x", u, k, h))
        source = lax.rem(x + 4 - h, 4)
        src = b.at[u, k, rows_of(source, SUB // 2 if h == 3 else 0, SUB // 2)]
        send(("xx", u, k, h), src, src, at(dx=h))
        src = b.at[u, k, rows_of(source)]
        send(("c", u, k, h), src, src, at(dc=1))

    def last(u, k, h):
        got(("xx", u, k, h))
        src = b.at[u, k, rows_of(lax.rem(x + 2, 4), SUB // 2 if h == 3 else 0, SUB // 2)]
        send(("c", u, k, h + 1), src, src, at(dc=1))

    def side(u, hh):
        if u == 0:
            got(("zero",))
        src = tile(u, pl.ds(hh * HALF, HALF))
        send(("z", u, hh, 1), src, src, at(dz=1))
        send(("z", u, hh, 3), src, src, at(dz=3))

    def side_on(u, hh, h):
        got(("z", u, hh, h))
        where = pl.ds(hh * HALF + (SUB if h == 3 else 0), SUB)
        src = a.at[u, where, lanes(lax.rem(z + 4 - h, 4))]
        send(("zz", u, hh, h), src, src, at(dz=h))

    def half_rows(hh):
        return pl.ds(hh * HALF, HALF)

    def product(left_unit, right_unit, k, hh):
        for h in (1, 3):
            got(("z", left_unit, hh, h), ("zz", left_unit, hh, h))
            got(("x", right_unit, k, h), ("xx", right_unit, k, h))
        got(("t", right_unit, k), *(("c", right_unit, k, i) for i in range(5)))
        return jnp.dot(a[left_unit, half_rows(hh)], b[right_unit, k], preferred_element_type=F32)

    def sq(s, k, hh):
        total[0, k, half_rows(hh)] = product(2 * s, 2 * s, k, hh)

    def cra(s, k, hh):
        total[1, k, half_rows(hh)] = product(2 * s + 1, 2 * s, k, hh)

    def crb(s, k, hh):
        total[1, k, half_rows(hh)] += product(2 * s, 2 * s + 1, k, hh)

    def reuse(kind, r, hh, h):
        if r > 1:
            gone((kind, r - 2, hh, h))

    def send_far(r, hh):
        p, where = r % 2, half_rows(hh)
        for h in (1, 3):
            reuse("s2", r, hh, h)
        part[p, 1, where] = total[p, 2, where].astype(BF)
        for h in (1, 3):
            where = pl.ds(hh * HALF + h // 2 * SUB, SUB)
            send(("s2", r, hh, h), part.at[p, 1, where], far.at[r, where], at(dy=h))

    def free(r, hh, h):
        p, i, where = r % 2, h // 2, pl.ds(hh * HALF + (1 - h // 2) * SUB, SUB)
        reuse("sf", r, hh, h)
        part[p, 2 * i, where] = total[p, h, where].astype(BF)
        send(("sf", r, hh, h), part.at[p, 2 * i, where], near.at[r, i, where], at(dy=h))

    def dep(r, hh, h):
        p, i, where = r % 2, h // 2, pl.ds(hh * HALF + h // 2 * SUB, SUB)
        reuse("sd", r, hh, h)
        got(("s2", r, hh, h))
        part[p, 2 * i, where] = (total[p, h, where] + far[r, where].astype(F32)).astype(BF)
        send(("sd", r, hh, h), part.at[p, 2 * i, where], near.at[r, i, where], at(dy=h))

    def keep(which, i, j):
        big_row, big_col = row * (TR // BLK) + i, col * (TC // BLK) + j
        return jnp.where(big_row == big_col, 1, patterns[which, big_row, big_col]).astype(F32)

    inv_root = 1.0 / math.sqrt(6144)

    def finish(r, hh):
        got(("patterns",))
        p = r % 2
        got(*((kind, r, hh, h) for kind in ("sf", "sd") for h in (1, 3)))

        @pl.loop(hh * (HALF // BLK), (hh + 1) * (HALF // BLK))
        def _(i):
            where = pl.ds(pl.multiple_of(i * BLK, BLK), BLK)
            for j in range(TC // BLK):
                cs = slice(j * BLK, (j + 1) * BLK)
                mine = pl.ds(pl.multiple_of(z * TC + j * BLK, BLK), BLK)
                value = (
                    total[p, 0, where, cs]
                    + near[r, 0, where, cs].astype(F32)
                    + near[r, 1, where, cs].astype(F32)
                ) * inv_root
                if r < 2:
                    a[r + 2, where, mine] = (keep(p, i, j) * value).astype(BF)
                else:
                    value = 2.0 * a[r, where, mine].astype(F32) - value
                    out[p, where, cs] = keep(p, i, j) * value

        if r > 1:
            where = half_rows(hh)
            move(("out", p, hh), out.at[p, where], (out_zero, out_first)[p].at[where])

    def iota(shape, dim):
        return lax.broadcasted_iota(I32, shape, dim)

    def ones(condition):
        return jnp.where(condition, 1.0, 0.0).astype(BF)

    def strips_place():
        square = (ITEMS, ITEMS)

        def across(ref):
            return jnp.broadcast_to(ref[...].astype(F32), square)

        named, own_name = across(dest), across(dest).T
        earlier = (named == own_name) & (iota(square, 1) < iota(square, 0))
        rank = jnp.sum(jnp.where(earlier, 1.0, 0.0), axis=1, keepdims=True)
        place = (own_name[:, 0:1] * 2.0 + rank).astype(I32)
        lane = iota(square, 1)
        tags = jnp.where(
            lane == 0, across(atoms).T + 1.0, jnp.where(lane == 1, across(blocks).T, 0.0)
        )
        rows[:, ATOM * BLK :] = tags.astype(BF)
        spread = ones(iota((ITEMS, SLOTS), 1) == place)
        got(("strips",))
        placed[0 : ITEMS * ATOM] = strips[...].astype(F32)
        for i in range(ATOM):
            lines = placed[pl.ds(i, ITEMS, stride=ATOM), :]
            rows[:, i * BLK : (i + 1) * BLK] = lines.astype(BF)
        sent[0] = lax.dot_general(
            spread, rows[...], (((0,), (0,)), ((), ())), preferred_element_type=F32
        ).astype(BF)

    def strips_x():
        mine = rows_at(row, 32)
        for dx in (2, 1, 3, 0):
            for dc in (0, 1):
                if dx or dc:
                    target = lax.rem(x + dx, 4) * 2 + lax.rem(core + dc, 2)
                    src = sent.at[0, rows_at(target, 32)]
                    send(("gx", dx, dc), src, came.at[0, mine], at(dx=dx, dc=dc))
        move(("gx", 0, 0), sent.at[0, mine], came.at[0, mine])

    def strips_col():
        got(*(("gx", dx, dc) for dx in range(4) for dc in range(2)))
        o = iota((SLOTS, SLOTS), 0)
        source = ((o >> 1) & 7) * 32 + (o >> 4) * 2 + (o & 1)
        taken = ones(iota((SLOTS, SLOTS), 1) == source)
        sent[1] = jnp.dot(taken, came[0], preferred_element_type=F32).astype(BF)
        mine = rows_at(col, 16)
        for dz in (2, 1, 3, 0):
            for dy in (2, 1, 3, 0):
                if dz or dy:
                    target = lax.rem(z + dz, 4) * 4 + lax.rem(y + dy, 4)
                    src = sent.at[1, rows_at(target, 16)]
                    send(("gc", dz, dy), src, came.at[1, mine], at(dz=dz, dy=dy))
        move(("gc", 0, 0), sent.at[1, mine], came.at[1, mine])

    def field():
        got(("patterns",))
        got(*(("gc", dz, dy) for dz in range(4) for dy in range(4)))
        tags = came[1, :, ATOM * BLK :].astype(F32)
        atom, block = tags[:, 0:1], tags[:, 1:2]
        cell = jnp.where(atom > 0.0, block * ATOMS + atom - 1.0, -1.0)
        placing = ones(iota((SLOTS, TC), 1).astype(F32) == cell)
        summed = lax.dot_general(
            placing, came[1, :, : ATOM * BLK], (((0,), (0,)), ((), ())), preferred_element_type=F32
        )
        for j in range(TC // BLK):
            for i in range(ATOM):
                placed[pl.ds(j * TR + i, ATOMS, stride=ATOM), :] = summed[
                    j * ATOMS : (j + 1) * ATOMS, i * BLK : (i + 1) * BLK
                ]

        @pl.loop(0, TR // BLK)
        def _(i):
            where = pl.ds(pl.multiple_of(i * BLK, BLK), BLK)
            for j in range(TC // BLK):
                mine = pl.ds(pl.multiple_of(z * TC + j * BLK, BLK), BLK)
                value = keep(2, i, j) * placed[pl.ds(pl.multiple_of(j * TR + i * BLK, BLK), BLK), :]
                a[1, where, mine] = (-value).astype(BF)

    move(("strips",), strips_hbm, strips)
    move(("zero",), zero_hbm, tile(0))
    move(("patterns",), patterns_hbm, patterns)
    peers = [at(dx=dx, dc=dc) for dx in range(4) for dc in range(2) if dx or dc]
    peers += [at(dz=dz, dy=dy) for dz in range(4) for dy in range(4) if dz or dy]
    peers += [at(dy=dy, dc=1) for dy in (1, 2, 3)]
    barrier = pltpu.get_barrier_semaphore()
    for peer in peers:
        pl.semaphore_signal(barrier, inc=1, device_id=peer, device_id_type=MESH)
    strips_place()
    pl.semaphore_wait(barrier, len(peers))

    turn(0, 0)
    strips_x()
    side(0, 0)
    turn(0, 1)
    own(0, 2)
    strips_col()
    side(0, 1)
    side_on(0, 0, 1)
    own(0, 0)
    own(0, 3)
    side_on(0, 0, 3)
    fwd(0, 2, 1)
    fwd(0, 2, 3)
    own(0, 1)
    field()
    turn(1, 1)
    fwd(0, 0, 3)
    fwd(0, 3, 1)
    turn(1, 0)
    fwd(0, 0, 1)
    fwd(0, 3, 3)
    last(0, 2, 3)
    side_on(0, 1, 1)
    fwd(0, 1, 1)
    side_on(0, 1, 3)
    side(1, 1)
    fwd(0, 1, 3)
    last(0, 2, 1)
    sq(0, 2, 0)
    send_far(0, 0)
    last(0, 1, 1)
    last(0, 3, 1)
    own(1, 2)
    last(0, 1, 3)
    last(0, 3, 3)
    side(1, 0)
    sq(0, 2, 1)
    send_far(0, 1)
    own(1, 3)
    sq(0, 1, 0)
    sq(0, 3, 0)
    last(0, 0, 3)
    free(0, 0, 3)
    free(0, 0, 1)
    own(1, 0)
    sq(0, 3, 1)
    dep(0, 0, 3)
    dep(0, 0, 1)
    last(0, 0, 1)
    side_on(1, 1, 1)
    sq(0, 1, 1)
    fwd(1, 2, 1)
    dep(0, 1, 1)
    side_on(1, 1, 3)
    sq(0, 0, 0)
    dep(0, 1, 3)
    fwd(1, 2, 3)
    fwd(1, 3, 1)
    sq(0, 0, 1)
    fwd(1, 3, 3)
    free(0, 1, 1)
    fwd(1, 0, 1)
    own(1, 1)
    side_on(1, 0, 3)
    free(0, 1, 3)
    finish(0, 0)
    turn(2, 0)
    last(1, 2, 3)
    last(1, 2, 1)
    side_on(1, 0, 1)
    last(1, 3, 3)
    side(2, 0)
    cra(0, 2, 1)
    crb(0, 2, 1)
    cra(0, 1, 1)
    last(1, 3, 1)
    send_far(1, 1)
    fwd(1, 1, 3)
    fwd(1, 1, 1)
    finish(0, 1)
    turn(2, 1)
    fwd(1, 0, 3)
    cra(0, 1, 0)
    cra(0, 2, 0)
    crb(0, 2, 0)
    send_far(1, 0)
    side(2, 1)
    last(1, 1, 3)
    cra(0, 3, 1)
    last(1, 1, 1)
    crb(0, 3, 1)
    crb(0, 1, 1)
    cra(0, 0, 0)
    free(1, 1, 3)
    dep(1, 1, 1)
    own(2, 2)
    dep(1, 1, 3)
    cra(0, 0, 1)
    cra(0, 3, 0)
    last(1, 0, 3)
    own(2, 1)
    free(1, 1, 1)
    side_on(2, 0, 1)
    crb(0, 1, 0)
    side_on(2, 1, 3)
    free(1, 0, 1)
    crb(0, 3, 0)
    last(1, 0, 1)
    free(1, 0, 3)
    side_on(2, 0, 3)
    dep(1, 0, 1)
    dep(1, 0, 3)
    own(2, 3)
    fwd(2, 2, 1)
    fwd(2, 2, 3)
    crb(0, 0, 1)
    side_on(2, 1, 1)
    fwd(2, 1, 3)
    finish(1, 1)
    turn(3, 1)
    side(3, 1)
    fwd(2, 1, 1)
    crb(0, 0, 0)
    last(2, 2, 3)
    fwd(2, 3, 3)
    own(2, 0)
    last(2, 2, 1)
    last(2, 1, 1)
    last(2, 1, 3)
    finish(1, 0)
    turn(3, 0)
    fwd(2, 3, 1)
    sq(1, 2, 0)
    sq(1, 1, 1)
    send_far(2, 0)
    side(3, 0)
    side_on(3, 1, 3)
    sq(1, 1, 0)
    sq(1, 2, 1)
    last(2, 3, 3)
    last(2, 3, 1)
    send_far(2, 1)
    own(3, 2)
    sq(1, 3, 1)
    sq(1, 3, 0)
    free(2, 0, 3)
    free(2, 0, 1)
    free(2, 1, 3)
    own(3, 3)
    dep(2, 0, 1)
    free(2, 1, 1)
    side_on(3, 1, 1)
    fwd(3, 2, 1)
    dep(2, 0, 3)
    fwd(3, 2, 3)
    own(3, 1)
    fwd(2, 0, 3)
    dep(2, 1, 1)
    side_on(3, 0, 1)
    side_on(3, 0, 3)
    dep(2, 1, 3)
    cra(1, 2, 1)
    last(3, 2, 3)
    fwd(3, 3, 1)
    cra(1, 3, 1)
    last(3, 2, 1)
    cra(1, 1, 1)
    fwd(3, 3, 3)
    crb(1, 2, 1)
    fwd(3, 1, 1)
    fwd(3, 1, 3)
    own(3, 0)
    cra(1, 1, 0)
    send_far(3, 1)
    cra(1, 2, 0)
    cra(1, 3, 0)
    last(3, 3, 1)
    last(3, 3, 3)
    crb(1, 2, 0)
    last(3, 1, 3)
    fwd(2, 0, 1)
    last(3, 1, 1)
    send_far(3, 0)
    last(2, 0, 3)
    crb(1, 3, 1)
    free(3, 1, 3)
    crb(1, 1, 0)
    fwd(3, 0, 3)
    free(3, 0, 1)
    crb(1, 3, 0)
    free(3, 0, 3)
    last(2, 0, 1)
    crb(1, 1, 1)
    free(3, 1, 1)
    dep(3, 0, 3)
    sq(1, 0, 1)
    cra(1, 0, 0)
    dep(3, 1, 3)
    fwd(3, 0, 1)
    dep(3, 0, 1)
    finish(2, 1)
    cra(1, 0, 1)
    last(3, 0, 3)
    dep(3, 1, 1)
    sq(1, 0, 0)
    finish(2, 0)
    last(3, 0, 1)
    crb(1, 0, 1)
    crb(1, 0, 0)
    finish(3, 0)
    finish(3, 1)

    got(*(name for name in moves if name[0] == "out"))
    gone(*copies)


def hand_on(zero, first, out_zero, out_first, held, in_sem, out_sem):
    ins, outs = [], []
    for i in range(4):
        where = pl.ds(i * SUB, SUB)
        for p, (src, dst) in enumerate(((zero, out_zero), (first, out_first))):
            n, slot = len(ins), held.at[p, where]
            ins.append(pltpu.make_async_copy(src.at[where], slot, in_sem.at[n]))
            outs.append(pltpu.make_async_copy(slot, dst.at[where], out_sem.at[n]))
            ins[n].start()
    for arrive, leave in zip(ins, outs):
        arrive.wait()
        leave.start()
    for leave in outs:
        leave.wait()


def on_device(density, strips, dest_device, atom_slot, block_slot, patterns):
    out = jax.ShapeDtypeStruct((TR, TC), F32)
    vmem = pl.BlockSpec(memory_space=pltpu.VMEM)
    hbm = pl.BlockSpec(memory_space=pl.ANY)
    results = pl.pallas_call(
        kernel,
        out_shape=(out, out),
        in_specs=[
            hbm, hbm, vmem, vmem, vmem, hbm,
        ],
        out_specs=(hbm, hbm),
        scratch_shapes=[
            pltpu.VMEM((4, TR, KB), BF),
            pltpu.VMEM((4, 4, KB, TC), BF),
            pltpu.VMEM((2, 4, TR, TC), F32),
            pltpu.VMEM((2, 3, TR, TC), BF),
            pltpu.VMEM((4, 2, TR, TC), BF),
            pltpu.VMEM((4, TR, TC), BF),
            pltpu.VMEM((ITEMS, WIDE), BF),
            pltpu.VMEM((2, SLOTS, WIDE), BF),
            pltpu.VMEM((2, SLOTS, WIDE), BF),
            pltpu.VMEM((TC // BLK * TR, BLK), F32),
            pltpu.VMEM((ITEMS * ATOM, BLK), BF),
            pltpu.SMEM((3, 48, 48), I32),
            pltpu.VMEM((2, TR, TC), F32),
            pltpu.SemaphoreType.DMA((N_COPIES,)),
            pltpu.SemaphoreType.DMA((N_COPIES,)),
            pltpu.SemaphoreType.DMA((16,)),
        ],
        compiler_params=pltpu.CompilerParams(
            collective_id=0, has_side_effects=True, vmem_limit_bytes=62 * 2**20 - 2**19
        ),
        cost_estimate=pl.CostEstimate(flops=21743271936, bytes_accessed=8 * 2**20, transcendentals=0),
    )(
        density,
        strips.reshape(ITEMS * ATOM, BLK),
        dest_device.reshape(1, ITEMS),
        atom_slot.reshape(1, ITEMS),
        block_slot.reshape(1, ITEMS),
        patterns,
    )
    return tuple(pl.pallas_call(
        hand_on,
        out_shape=(out, out),
        in_specs=(hbm, hbm),
        out_specs=(hbm, hbm),
        scratch_shapes=[
            pltpu.VMEM((2, TR, TC), F32),
            pltpu.SemaphoreType.DMA((8,)),
            pltpu.SemaphoreType.DMA((8,)),
        ],
    )(*results))


def solution(mesh):
    return jax.shard_map(
        on_device,
        mesh=mesh,
        in_specs=(
            P("row", "col"),
            P(("row", "col"), None, None),
            P(("row", "col"), None),
            P(("row", "col")),
            P(("row", "col")),
            P(),
        ),
        out_specs=(P("row", "col"), P("row", "col")),
        check_vma=False,
    )
```

```python
import math

import jax
import jax.numpy as jnp
from jax import lax
from jax.experimental import pallas as pl
from jax.experimental.pallas import tpu as pltpu
from jax.sharding import PartitionSpec as P

MESH = pl.DeviceIdType.MESH
BF = jnp.bfloat16
F32 = jnp.float32
I32 = jnp.int32
TR, TC = 768, 384
HALF = TR // 2
KB = 1536
SUB = TR // 4
BLK = 128
ATOM = 8
ITEMS = 128
SLOTS = 256
WIDE = ATOM * BLK + BLK
ATOMS = TR // ATOM
N_COPIES = 272


def kernel(
    zero_hbm, strips_hbm, dest, atoms, blocks, patterns_hbm, out_zero, out_first,
    a, b, total, part, near, far, rows, sent, came, placed, strips, patterns, out, send_sem, recv_sem, local_sem,
):
    row, col = lax.axis_index("row"), lax.axis_index("col")
    x, core = row // 2, row % 2
    z, y = col // 4, col % 4

    def at(dx=0, dz=0, dy=0, dc=0):
        nx, nz, ny = (lax.rem(x + dx, 4), lax.rem(z + dz, 4), lax.rem(y + dy, 4))
        return {"row": nx * 2 + lax.rem(core + dc, 2), "col": nz * 4 + ny}

    copies, moves, turns, bases, away = {}, {}, {}, {}, {}
    arrived, left = set(), set()
    used = [0]

    def take(n):
        used[0] += n
        return used[0] - n

    def send(name, src, dst, device):
        i = take(1)
        copies[name] = pltpu.make_async_remote_copy(
            src_ref=src, dst_ref=dst, send_sem=send_sem.at[i], recv_sem=recv_sem.at[i],
            device_id=device, device_id_type=MESH,
        )
        copies[name].start()

    def move(name, src, dst):
        moves[name] = pltpu.make_async_copy(src, dst, local_sem.at[len(moves)])
        moves[name].start()

    def got(*names):
        for name in names:
            if name not in arrived:
                arrived.add(name)
                if name[0] == "t":
                    turns[name].wait_recv()
                elif name in copies:
                    copies[name].wait_recv()
                else:
                    moves[name].wait()

    def gone(*names):
        for name in names:
            if name not in left:
                left.add(name)
                if name[0] == "t" and name[3] == 0:
                    pl.when(away[name])(copies[name].wait_send)
                else:
                    copies[name].wait_send()

    def lanes(position):
        return pl.ds(pl.multiple_of(position * TC, BLK), TC)

    def rows_of(position, first=0, size=SUB):
        return pl.ds(pl.multiple_of(position * TC + core * SUB + first, 32), size)

    def rows_at(position, size):
        return pl.ds(pl.multiple_of(position * size, 16), size)

    def tile(u, where=slice(None)):
        return a.at[u, where, lanes(z)]

    def turn(u, hh):
        if u == 0:
            got(("zero",))
        if ("t", u, 0) not in turns:
            base = take(4)
            for k in range(4):
                dst = b.at[u, k, rows_of(x)]
                turns["t", u, k] = pltpu.make_async_remote_copy(
                    src_ref=dst, dst_ref=dst, send_sem=send_sem.at[base],
                    recv_sem=recv_sem.at[base + k], device_id=at(dc=1), device_id_type=MESH,
                )
            bases[u] = base
        base = bases[u]
        quarter = 2 * core + hh
        k = lax.rem(y - quarter + 4, 4)
        for e in (1, 0):
            d = lax.rem(core + e, 2)
            src = tile(u, pl.ds(pl.multiple_of(hh * TC + d * SUB, 32), SUB))
            dst = b.at[u, k, pl.ds(pl.multiple_of(x * TC + d * SUB, 32), SUB)]
            name = ("t", u, hh, e)
            copies[name] = pltpu.make_async_remote_copy(
                src_ref=src, dst_ref=dst, send_sem=send_sem.at[base + 2 * hh + e],
                recv_sem=recv_sem.at[base + k],
                device_id={"row": x * 2 + d, "col": z * 4 + quarter}, device_id_type=MESH,
            )
            if e == 0:
                away[name] = quarter != y
                pl.when(quarter != y)(copies[name].start)
                here = pltpu.make_async_copy(src, dst, recv_sem.at[base + k])
                pl.when(quarter == y)(here.start)
            else:
                copies[name].start()

    def own(u, k):
        got(("t", u, k))
        src = b.at[u, k, rows_of(x)]
        send(("x", u, k, 1), src, src, at(dx=1))
        send(("x", u, k, 3), src, src, at(dx=3))
        send(("c", u, k, 0), src, src, at(dc=1))

    def fwd(u, k, h):
        got(("x", u, k, h))
        source = lax.rem(x + 4 - h, 4)
        src = b.at[u, k, rows_of(source, SUB // 2 if h == 3 else 0, SUB // 2)]
        send(("xx", u, k, h), src, src, at(dx=h))
        src = b.at[u, k, rows_of(source)]
        send(("c", u, k, h), src, src, at(dc=1))

    def last(u, k, h):
        got(("xx", u, k, h))
        src = b.at[u, k, rows_of(lax.rem(x + 2, 4), SUB // 2 if h == 3 else 0, SUB // 2)]
        send(("c", u, k, h + 1), src, src, at(dc=1))

    def side(u, hh):
        if u == 0:
            got(("zero",))
        src = tile(u, pl.ds(hh * HALF, HALF))
        send(("z", u, hh, 1), src, src, at(dz=1))
        send(("z", u, hh, 3), src, src, at(dz=3))

    def side_on(u, hh, h):
        got(("z", u, hh, h))
        where = pl.ds(hh * HALF + (SUB if h == 3 else 0), SUB)
        src = a.at[u, where, lanes(lax.rem(z + 4 - h, 4))]
        send(("zz", u, hh, h), src, src, at(dz=h))

    def half_rows(hh):
        return pl.ds(hh * HALF, HALF)

    def product(left_unit, right_unit, k, hh):
        for h in (1, 3):
            got(("z", left_unit, hh, h), ("zz", left_unit, hh, h))
            got(("x", right_unit, k, h), ("xx", right_unit, k, h))
        got(("t", right_unit, k), *(("c", right_unit, k, i) for i in range(5)))
        return jnp.dot(a[left_unit, half_rows(hh)], b[right_unit, k], preferred_element_type=F32)

    def sq(s, k, hh):
        total[0, k, half_rows(hh)] = product(2 * s, 2 * s, k, hh)

    def cra(s, k, hh):
        total[1, k, half_rows(hh)] = product(2 * s + 1, 2 * s, k, hh)

    def crb(s, k, hh):
        total[1, k, half_rows(hh)] += product(2 * s, 2 * s + 1, k, hh)

    def reuse(kind, r, hh, h):
        if r > 1:
            gone((kind, r - 2, hh, h))

    def send_far(r, hh):
        p, where = r % 2, half_rows(hh)
        for h in (1, 3):
            reuse("s2", r, hh, h)
        part[p, 1, where] = total[p, 2, where].astype(BF)
        for h in (1, 3):
            where = pl.ds(hh * HALF + h // 2 * SUB, SUB)
            send(("s2", r, hh, h), part.at[p, 1, where], far.at[r, where], at(dy=h))

    def free(r, hh, h):
        p, i, where = r % 2, h // 2, pl.ds(hh * HALF + (1 - h // 2) * SUB, SUB)
        reuse("sf", r, hh, h)
        part[p, 2 * i, where] = total[p, h, where].astype(BF)
        send(("sf", r, hh, h), part.at[p, 2 * i, where], near.at[r, i, where], at(dy=h))

    def dep(r, hh, h):
        p, i, where = r % 2, h // 2, pl.ds(hh * HALF + h // 2 * SUB, SUB)
        reuse("sd", r, hh, h)
        got(("s2", r, hh, h))
        part[p, 2 * i, where] = (total[p, h, where] + far[r, where].astype(F32)).astype(BF)
        send(("sd", r, hh, h), part.at[p, 2 * i, where], near.at[r, i, where], at(dy=h))

    def keep(which, i, j):
        big_row, big_col = row * (TR // BLK) + i, col * (TC // BLK) + j
        return jnp.where(big_row == big_col, 1, patterns[which, big_row, big_col]).astype(F32)

    inv_root = 1.0 / math.sqrt(6144)

    def finish(r, hh):
        got(("patterns",))
        p = r % 2
        got(*((kind, r, hh, h) for kind in ("sf", "sd") for h in (1, 3)))

        @pl.loop(hh * (HALF // BLK), (hh + 1) * (HALF // BLK))
        def _(i):
            where = pl.ds(pl.multiple_of(i * BLK, BLK), BLK)
            for j in range(TC // BLK):
                cs = slice(j * BLK, (j + 1) * BLK)
                mine = pl.ds(pl.multiple_of(z * TC + j * BLK, BLK), BLK)
                value = (
                    total[p, 0, where, cs]
                    + near[r, 0, where, cs].astype(F32)
                    + near[r, 1, where, cs].astype(F32)
                ) * inv_root
                if r < 2:
                    a[r + 2, where, mine] = (keep(p, i, j) * value).astype(BF)
                else:
                    value = 2.0 * a[r, where, mine].astype(F32) - value
                    out[p, where, cs] = keep(p, i, j) * value

        if r > 1:
            where = half_rows(hh)
            move(("out", p, hh), out.at[p, where], (out_zero, out_first)[p].at[where])

    def iota(shape, dim):
        return lax.broadcasted_iota(I32, shape, dim)

    def ones(condition):
        return jnp.where(condition, 1.0, 0.0).astype(BF)

    def strips_place():
        square = (ITEMS, ITEMS)

        def across(ref):
            return jnp.broadcast_to(ref[...].astype(F32), square)

        named, own_name = across(dest), across(dest).T
        earlier = (named == own_name) & (iota(square, 1) < iota(square, 0))
        rank = jnp.sum(jnp.where(earlier, 1.0, 0.0), axis=1, keepdims=True)
        place = (own_name[:, 0:1] * 2.0 + rank).astype(I32)
        lane = iota(square, 1)
        tags = jnp.where(
            lane == 0, across(atoms).T + 1.0, jnp.where(lane == 1, across(blocks).T, 0.0)
        )
        rows[:, ATOM * BLK :] = tags.astype(BF)
        spread = ones(iota((ITEMS, SLOTS), 1) == place)
        got(("strips",))
        placed[0 : ITEMS * ATOM] = strips[...].astype(F32)
        for i in range(ATOM):
            lines = placed[pl.ds(i, ITEMS, stride=ATOM), :]
            rows[:, i * BLK : (i + 1) * BLK] = lines.astype(BF)
        sent[0] = lax.dot_general(
            spread, rows[...], (((0,), (0,)), ((), ())), preferred_element_type=F32
        ).astype(BF)

    def strips_x():
        mine = rows_at(row, 32)
        for dx in (2, 1, 3, 0):
            for dc in (0, 1):
                if dx or dc:
                    target = lax.rem(x + dx, 4) * 2 + lax.rem(core + dc, 2)
                    src = sent.at[0, rows_at(target, 32)]
                    send(("gx", dx, dc), src, came.at[0, mine], at(dx=dx, dc=dc))
        move(("gx", 0, 0), sent.at[0, mine], came.at[0, mine])

    def strips_col():
        got(*(("gx", dx, dc) for dx in range(4) for dc in range(2)))
        o = iota((SLOTS, SLOTS), 0)
        source = ((o >> 1) & 7) * 32 + (o >> 4) * 2 + (o & 1)
        taken = ones(iota((SLOTS, SLOTS), 1) == source)
        sent[1] = jnp.dot(taken, came[0], preferred_element_type=F32).astype(BF)
        mine = rows_at(col, 16)
        for dz in (2, 1, 3, 0):
            for dy in (2, 1, 3, 0):
                if dz or dy:
                    target = lax.rem(z + dz, 4) * 4 + lax.rem(y + dy, 4)
                    src = sent.at[1, rows_at(target, 16)]
                    send(("gc", dz, dy), src, came.at[1, mine], at(dz=dz, dy=dy))
        move(("gc", 0, 0), sent.at[1, mine], came.at[1, mine])

    def field():
        got(("patterns",))
        got(*(("gc", dz, dy) for dz in range(4) for dy in range(4)))
        tags = came[1, :, ATOM * BLK :].astype(F32)
        atom, block = tags[:, 0:1], tags[:, 1:2]
        cell = jnp.where(atom > 0.0, block * ATOMS + atom - 1.0, -1.0)
        placing = ones(iota((SLOTS, TC), 1).astype(F32) == cell)
        summed = lax.dot_general(
            placing, came[1, :, : ATOM * BLK], (((0,), (0,)), ((), ())), preferred_element_type=F32
        )
        for j in range(TC // BLK):
            for i in range(ATOM):
                placed[pl.ds(j * TR + i, ATOMS, stride=ATOM), :] = summed[
                    j * ATOMS : (j + 1) * ATOMS, i * BLK : (i + 1) * BLK
                ]

        @pl.loop(0, TR // BLK)
        def _(i):
            where = pl.ds(pl.multiple_of(i * BLK, BLK), BLK)
            for j in range(TC // BLK):
                mine = pl.ds(pl.multiple_of(z * TC + j * BLK, BLK), BLK)
                value = keep(2, i, j) * placed[pl.ds(pl.multiple_of(j * TR + i * BLK, BLK), BLK), :]
                a[1, where, mine] = (-value).astype(BF)

    move(("strips",), strips_hbm, strips)
    move(("zero",), zero_hbm, tile(0))
    move(("patterns",), patterns_hbm, patterns)
    peers = [at(dx=dx, dc=dc) for dx in range(4) for dc in range(2) if dx or dc]
    peers += [at(dz=dz, dy=dy) for dz in range(4) for dy in range(4) if dz or dy]
    peers += [at(dy=dy, dc=1) for dy in (1, 2, 3)]
    barrier = pltpu.get_barrier_semaphore()
    for peer in peers:
        pl.semaphore_signal(barrier, inc=1, device_id=peer, device_id_type=MESH)
    strips_place()
    pl.semaphore_wait(barrier, len(peers))

    side(0, 0)
    turn(0, 0)
    side(0, 1)
    turn(0, 1)
    strips_x()
    own(0, 2)
    own(0, 1)
    strips_col()
    fwd(0, 2, 1)
    side_on(0, 1, 3)
    own(0, 3)
    side_on(0, 0, 3)
    side_on(0, 1, 1)
    fwd(0, 2, 3)
    fwd(0, 1, 1)
    last(0, 2, 1)
    own(0, 0)
    side_on(0, 0, 1)
    field()
    turn(1, 0)
    side(1, 1)
    last(0, 1, 1)
    fwd(0, 3, 3)
    last(0, 2, 3)
    fwd(0, 0, 3)
    fwd(0, 1, 3)
    fwd(0, 3, 1)
    turn(1, 1)
    side(1, 0)
    sq(0, 2, 1)
    send_far(0, 1)
    fwd(0, 0, 1)
    sq(0, 2, 0)
    send_far(0, 0)
    last(0, 3, 3)
    last(0, 3, 1)
    sq(0, 3, 1)
    last(0, 1, 3)
    own(1, 2)
    free(0, 1, 3)
    sq(0, 3, 0)
    side_on(1, 1, 3)
    side_on(1, 1, 1)
    sq(0, 1, 1)
    free(0, 1, 1)
    own(1, 1)
    dep(0, 1, 1)
    last(0, 0, 3)
    sq(0, 1, 0)
    own(1, 3)
    dep(0, 1, 3)
    free(0, 0, 1)
    dep(0, 0, 1)
    side_on(1, 0, 3)
    fwd(1, 2, 1)
    free(0, 0, 3)
    fwd(1, 2, 3)
    last(0, 0, 1)
    own(1, 0)
    dep(0, 0, 3)
    sq(0, 0, 0)
    side_on(1, 0, 1)
    fwd(1, 1, 1)
    sq(0, 0, 1)
    cra(0, 1, 1)
    finish(0, 1)
    fwd(1, 1, 3)
    cra(0, 3, 1)
    side(2, 1)
    turn(2, 1)
    last(1, 2, 1)
    last(1, 2, 3)
    fwd(1, 3, 3)
    cra(0, 2, 1)
    crb(0, 2, 1)
    send_far(1, 1)
    cra(0, 2, 0)
    fwd(1, 3, 1)
    last(1, 3, 3)
    finish(0, 0)
    turn(2, 0)
    last(1, 1, 1)
    last(1, 1, 3)
    fwd(1, 0, 3)
    side(2, 0)
    crb(0, 2, 0)
    crb(0, 1, 1)
    last(1, 3, 1)
    free(1, 1, 1)
    send_far(1, 0)
    side_on(2, 1, 1)
    cra(0, 1, 0)
    fwd(1, 0, 1)
    crb(0, 3, 1)
    dep(1, 1, 3)
    last(1, 0, 3)
    own(2, 1)
    own(2, 2)
    free(1, 1, 3)
    crb(0, 1, 0)
    dep(1, 1, 1)
    cra(0, 3, 0)
    side_on(2, 0, 1)
    last(1, 0, 1)
    crb(0, 3, 0)
    own(2, 3)
    free(1, 0, 3)
    side_on(2, 0, 3)
    dep(1, 0, 3)
    free(1, 0, 1)
    cra(0, 0, 1)
    crb(0, 0, 1)
    fwd(2, 1, 1)
    side_on(2, 1, 3)
    dep(1, 0, 1)
    fwd(2, 2, 3)
    finish(1, 1)
    fwd(2, 2, 1)
    side(3, 1)
    fwd(2, 1, 3)
    cra(0, 0, 0)
    turn(3, 1)
    fwd(2, 3, 1)
    crb(0, 0, 0)
    fwd(2, 3, 3)
    last(2, 1, 1)
    own(2, 0)
    last(2, 2, 3)
    last(2, 2, 1)
    finish(1, 0)
    turn(3, 0)
    last(2, 1, 3)
    sq(1, 2, 1)
    side(3, 0)
    send_far(2, 1)
    sq(1, 1, 0)
    last(2, 3, 1)
    sq(1, 2, 0)
    last(2, 3, 3)
    fwd(2, 0, 1)
    send_far(2, 0)
    side_on(3, 1, 1)
    sq(1, 1, 1)
    own(3, 2)
    sq(1, 3, 1)
    side_on(3, 1, 3)
    sq(1, 3, 0)
    free(2, 1, 3)
    own(3, 3)
    free(2, 1, 1)
    side_on(3, 0, 3)
    dep(2, 1, 3)
    dep(2, 1, 1)
    side_on(3, 0, 1)
    fwd(3, 2, 1)
    fwd(3, 2, 3)
    free(2, 0, 1)
    dep(2, 0, 1)
    free(2, 0, 3)
    own(3, 1)
    dep(2, 0, 3)
    cra(1, 2, 1)
    fwd(3, 3, 3)
    cra(1, 3, 1)
    last(3, 2, 1)
    last(3, 2, 3)
    fwd(3, 3, 1)
    cra(1, 2, 0)
    fwd(2, 0, 3)
    crb(1, 2, 1)
    send_far(3, 1)
    fwd(3, 1, 3)
    fwd(3, 1, 1)
    cra(1, 1, 0)
    own(3, 0)
    last(3, 3, 3)
    last(3, 3, 1)
    last(2, 0, 1)
    crb(1, 2, 0)
    send_far(3, 0)
    crb(1, 3, 1)
    last(3, 1, 1)
    last(3, 1, 3)
    cra(1, 1, 1)
    crb(1, 1, 1)
    free(3, 1, 1)
    free(3, 1, 3)
    fwd(3, 0, 1)
    dep(3, 1, 3)
    fwd(3, 0, 3)
    last(2, 0, 3)
    dep(3, 1, 1)
    cra(1, 3, 0)
    crb(1, 3, 0)
    dep(3, 0, 3)
    crb(1, 1, 0)
    free(3, 0, 3)
    dep(3, 0, 1)
    sq(1, 0, 0)
    cra(1, 0, 1)
    sq(1, 0, 1)
    free(3, 0, 1)
    last(3, 0, 1)
    finish(2, 1)
    last(3, 0, 3)
    cra(1, 0, 0)
    crb(1, 0, 0)
    crb(1, 0, 1)
    finish(3, 1)
    finish(2, 0)
    finish(3, 0)

    got(*(name for name in moves if name[0] == "out"))
    gone(*copies)


def hand_on(zero, first, out_zero, out_first, held, in_sem, out_sem):
    ins, outs = [], []
    for i in range(4):
        where = pl.ds(i * SUB, SUB)
        for p, (src, dst) in enumerate(((zero, out_zero), (first, out_first))):
            n, slot = len(ins), held.at[p, where]
            ins.append(pltpu.make_async_copy(src.at[where], slot, in_sem.at[n]))
            outs.append(pltpu.make_async_copy(slot, dst.at[where], out_sem.at[n]))
            ins[n].start()
    for arrive, leave in zip(ins, outs):
        arrive.wait()
        leave.start()
    for leave in outs:
        leave.wait()


def on_device(density, strips, dest_device, atom_slot, block_slot, patterns):
    out = jax.ShapeDtypeStruct((TR, TC), F32)
    vmem = pl.BlockSpec(memory_space=pltpu.VMEM)
    hbm = pl.BlockSpec(memory_space=pl.ANY)
    results = pl.pallas_call(
        kernel,
        out_shape=(out, out),
        in_specs=[
            hbm, hbm, vmem, vmem, vmem, hbm,
        ],
        out_specs=(hbm, hbm),
        scratch_shapes=[
            pltpu.VMEM((4, TR, KB), BF),
            pltpu.VMEM((4, 4, KB, TC), BF),
            pltpu.VMEM((2, 4, TR, TC), F32),
            pltpu.VMEM((2, 3, TR, TC), BF),
            pltpu.VMEM((4, 2, TR, TC), BF),
            pltpu.VMEM((4, TR, TC), BF),
            pltpu.VMEM((ITEMS, WIDE), BF),
            pltpu.VMEM((2, SLOTS, WIDE), BF),
            pltpu.VMEM((2, SLOTS, WIDE), BF),
            pltpu.VMEM((TC // BLK * TR, BLK), F32),
            pltpu.VMEM((ITEMS * ATOM, BLK), BF),
            pltpu.SMEM((3, 48, 48), I32),
            pltpu.VMEM((2, TR, TC), F32),
            pltpu.SemaphoreType.DMA((N_COPIES,)),
            pltpu.SemaphoreType.DMA((N_COPIES,)),
            pltpu.SemaphoreType.DMA((16,)),
        ],
        compiler_params=pltpu.CompilerParams(
            collective_id=0, has_side_effects=True, vmem_limit_bytes=62 * 2**20 - 2**19
        ),
        cost_estimate=pl.CostEstimate(flops=21743271936, bytes_accessed=8 * 2**20, transcendentals=0),
    )(
        density,
        strips.reshape(ITEMS * ATOM, BLK),
        dest_device.reshape(1, ITEMS),
        atom_slot.reshape(1, ITEMS),
        block_slot.reshape(1, ITEMS),
        patterns,
    )
    return tuple(pl.pallas_call(
        hand_on,
        out_shape=(out, out),
        in_specs=(hbm, hbm),
        out_specs=(hbm, hbm),
        scratch_shapes=[
            pltpu.VMEM((2, TR, TC), F32),
            pltpu.SemaphoreType.DMA((8,)),
            pltpu.SemaphoreType.DMA((8,)),
        ],
    )(*results))


def solution(mesh):
    return jax.shard_map(
        on_device,
        mesh=mesh,
        in_specs=(
            P("row", "col"),
            P(("row", "col"), None, None),
            P(("row", "col"), None),
            P(("row", "col")),
            P(("row", "col")),
            P(),
        ),
        out_specs=(P("row", "col"), P("row", "col")),
        check_vma=False,
    )
```

```python
import math

import jax
import jax.numpy as jnp
from jax import lax
from jax.experimental import pallas as pl
from jax.experimental.pallas import tpu as pltpu
from jax.sharding import PartitionSpec as P

MESH = pl.DeviceIdType.MESH
BF = jnp.bfloat16
F32 = jnp.float32
I32 = jnp.int32
TR, TC = 768, 384
HALF = TR // 2
KB = 1536
SUB = TR // 4
BLK = 128
ATOM = 8
ITEMS = 128
SLOTS = 256
WIDE = ATOM * BLK + BLK
ATOMS = TR // ATOM
N_COPIES = 272


def kernel(
    zero_hbm, strips_hbm, dest, atoms, blocks, patterns_hbm, out_zero, out_first,
    a, b, total, part, near, far, rows, sent, came, placed, strips, patterns, out, send_sem, recv_sem, local_sem,
):
    row, col = lax.axis_index("row"), lax.axis_index("col")
    x, core = row // 2, row % 2
    z, y = col // 4, col % 4

    def at(dx=0, dz=0, dy=0, dc=0):
        nx, nz, ny = (lax.rem(x + dx, 4), lax.rem(z + dz, 4), lax.rem(y + dy, 4))
        return {"row": nx * 2 + lax.rem(core + dc, 2), "col": nz * 4 + ny}

    copies, moves, turns, bases, away = {}, {}, {}, {}, {}
    arrived, left = set(), set()
    used = [0]

    def take(n):
        used[0] += n
        return used[0] - n

    def send(name, src, dst, device):
        i = take(1)
        copies[name] = pltpu.make_async_remote_copy(
            src_ref=src, dst_ref=dst, send_sem=send_sem.at[i], recv_sem=recv_sem.at[i],
            device_id=device, device_id_type=MESH,
        )
        copies[name].start()

    def move(name, src, dst):
        moves[name] = pltpu.make_async_copy(src, dst, local_sem.at[len(moves)])
        moves[name].start()

    def got(*names):
        for name in names:
            if name not in arrived:
                arrived.add(name)
                if name[0] == "t":
                    turns[name].wait_recv()
                elif name in copies:
                    copies[name].wait_recv()
                else:
                    moves[name].wait()

    def gone(*names):
        for name in names:
            if name not in left:
                left.add(name)
                if name[0] == "t" and name[3] == 0:
                    pl.when(away[name])(copies[name].wait_send)
                else:
                    copies[name].wait_send()

    def lanes(position):
        return pl.ds(pl.multiple_of(position * TC, BLK), TC)

    def rows_of(position, first=0, size=SUB):
        return pl.ds(pl.multiple_of(position * TC + core * SUB + first, 32), size)

    def rows_at(position, size):
        return pl.ds(pl.multiple_of(position * size, 16), size)

    def tile(u, where=slice(None)):
        return a.at[u, where, lanes(z)]

    def turn(u, hh):
        if u == 0:
            got(("zero",))
        if ("t", u, 0) not in turns:
            base = take(4)
            for k in range(4):
                dst = b.at[u, k, rows_of(x)]
                turns["t", u, k] = pltpu.make_async_remote_copy(
                    src_ref=dst, dst_ref=dst, send_sem=send_sem.at[base],
                    recv_sem=recv_sem.at[base + k], device_id=at(dc=1), device_id_type=MESH,
                )
            bases[u] = base
        base = bases[u]
        quarter = 2 * core + hh
        k = lax.rem(y - quarter + 4, 4)
        for e in (1, 0):
            d = lax.rem(core + e, 2)
            src = tile(u, pl.ds(pl.multiple_of(hh * TC + d * SUB, 32), SUB))
            dst = b.at[u, k, pl.ds(pl.multiple_of(x * TC + d * SUB, 32), SUB)]
            name = ("t", u, hh, e)
            copies[name] = pltpu.make_async_remote_copy(
                src_ref=src, dst_ref=dst, send_sem=send_sem.at[base + 2 * hh + e],
                recv_sem=recv_sem.at[base + k],
                device_id={"row": x * 2 + d, "col": z * 4 + quarter}, device_id_type=MESH,
            )
            if e == 0:
                away[name] = quarter != y
                pl.when(quarter != y)(copies[name].start)
                here = pltpu.make_async_copy(src, dst, recv_sem.at[base + k])
                pl.when(quarter == y)(here.start)
            else:
                copies[name].start()

    def own(u, k):
        got(("t", u, k))
        src = b.at[u, k, rows_of(x)]
        send(("x", u, k, 1), src, src, at(dx=1))
        send(("x", u, k, 3), src, src, at(dx=3))
        send(("c", u, k, 0), src, src, at(dc=1))

    def fwd(u, k, h):
        got(("x", u, k, h))
        source = lax.rem(x + 4 - h, 4)
        src = b.at[u, k, rows_of(source, SUB // 2 if h == 3 else 0, SUB // 2)]
        send(("xx", u, k, h), src, src, at(dx=h))
        src = b.at[u, k, rows_of(source)]
        send(("c", u, k, h), src, src, at(dc=1))

    def last(u, k, h):
        got(("xx", u, k, h))
        src = b.at[u, k, rows_of(lax.rem(x + 2, 4), SUB // 2 if h == 3 else 0, SUB // 2)]
        send(("c", u, k, h + 1), src, src, at(dc=1))

    def side(u, hh):
        if u == 0:
            got(("zero",))
        src = tile(u, pl.ds(hh * HALF, HALF))
        send(("z", u, hh, 1), src, src, at(dz=1))
        send(("z", u, hh, 3), src, src, at(dz=3))

    def side_on(u, hh, h):
        got(("z", u, hh, h))
        where = pl.ds(hh * HALF + (SUB if h == 3 else 0), SUB)
        src = a.at[u, where, lanes(lax.rem(z + 4 - h, 4))]
        send(("zz", u, hh, h), src, src, at(dz=h))

    def half_rows(hh):
        return pl.ds(hh * HALF, HALF)

    def product(left_unit, right_unit, k, hh):
        for h in (1, 3):
            got(("z", left_unit, hh, h), ("zz", left_unit, hh, h))
            got(("x", right_unit, k, h), ("xx", right_unit, k, h))
        got(("t", right_unit, k), *(("c", right_unit, k, i) for i in range(5)))
        return jnp.dot(a[left_unit, half_rows(hh)], b[right_unit, k], preferred_element_type=F32)

    def sq(s, k, hh):
        total[0, k, half_rows(hh)] = product(2 * s, 2 * s, k, hh)

    def cra(s, k, hh):
        total[1, k, half_rows(hh)] = product(2 * s + 1, 2 * s, k, hh)

    def crb(s, k, hh):
        total[1, k, half_rows(hh)] += product(2 * s, 2 * s + 1, k, hh)

    def reuse(kind, r, hh, h):
        if r > 1:
            gone((kind, r - 2, hh, h))

    def send_far(r, hh):
        p, where = r % 2, half_rows(hh)
        for h in (1, 3):
            reuse("s2", r, hh, h)
        part[p, 1, where] = total[p, 2, where].astype(BF)
        for h in (1, 3):
            where = pl.ds(hh * HALF + h // 2 * SUB, SUB)
            send(("s2", r, hh, h), part.at[p, 1, where], far.at[r, where], at(dy=h))

    def free(r, hh, h):
        p, i, where = r % 2, h // 2, pl.ds(hh * HALF + (1 - h // 2) * SUB, SUB)
        reuse("sf", r, hh, h)
        part[p, 2 * i, where] = total[p, h, where].astype(BF)
        send(("sf", r, hh, h), part.at[p, 2 * i, where], near.at[r, i, where], at(dy=h))

    def dep(r, hh, h):
        p, i, where = r % 2, h // 2, pl.ds(hh * HALF + h // 2 * SUB, SUB)
        reuse("sd", r, hh, h)
        got(("s2", r, hh, h))
        part[p, 2 * i, where] = (total[p, h, where] + far[r, where].astype(F32)).astype(BF)
        send(("sd", r, hh, h), part.at[p, 2 * i, where], near.at[r, i, where], at(dy=h))

    def keep(which, i, j):
        big_row, big_col = row * (TR // BLK) + i, col * (TC // BLK) + j
        return jnp.where(big_row == big_col, 1, patterns[which, big_row, big_col]).astype(F32)

    inv_root = 1.0 / math.sqrt(6144)

    def finish(r, hh):
        got(("patterns",))
        p = r % 2
        got(*((kind, r, hh, h) for kind in ("sf", "sd") for h in (1, 3)))

        @pl.loop(hh * (HALF // BLK), (hh + 1) * (HALF // BLK))
        def _(i):
            where = pl.ds(pl.multiple_of(i * BLK, BLK), BLK)
            for j in range(TC // BLK):
                cs = slice(j * BLK, (j + 1) * BLK)
                mine = pl.ds(pl.multiple_of(z * TC + j * BLK, BLK), BLK)
                value = (
                    total[p, 0, where, cs]
                    + near[r, 0, where, cs].astype(F32)
                    + near[r, 1, where, cs].astype(F32)
                ) * inv_root
                if r < 2:
                    a[r + 2, where, mine] = (keep(p, i, j) * value).astype(BF)
                else:
                    value = 2.0 * a[r, where, mine].astype(F32) - value
                    out[p, where, cs] = keep(p, i, j) * value

        if r > 1:
            where = half_rows(hh)
            move(("out", p, hh), out.at[p, where], (out_zero, out_first)[p].at[where])

    def iota(shape, dim):
        return lax.broadcasted_iota(I32, shape, dim)

    def ones(condition):
        return jnp.where(condition, 1.0, 0.0).astype(BF)

    def strips_place():
        square = (ITEMS, ITEMS)

        def across(ref):
            return jnp.broadcast_to(ref[...].astype(F32), square)

        named, own_name = across(dest), across(dest).T
        earlier = (named == own_name) & (iota(square, 1) < iota(square, 0))
        rank = jnp.sum(jnp.where(earlier, 1.0, 0.0), axis=1, keepdims=True)
        place = (own_name[:, 0:1] * 2.0 + rank).astype(I32)
        lane = iota(square, 1)
        tags = jnp.where(
            lane == 0, across(atoms).T + 1.0, jnp.where(lane == 1, across(blocks).T, 0.0)
        )
        rows[:, ATOM * BLK :] = tags.astype(BF)
        spread = ones(iota((ITEMS, SLOTS), 1) == place)
        got(("strips",))
        placed[0 : ITEMS * ATOM] = strips[...].astype(F32)
        for i in range(ATOM):
            lines = placed[pl.ds(i, ITEMS, stride=ATOM), :]
            rows[:, i * BLK : (i + 1) * BLK] = lines.astype(BF)
        sent[0] = lax.dot_general(
            spread, rows[...], (((0,), (0,)), ((), ())), preferred_element_type=F32
        ).astype(BF)

    def strips_x():
        mine = rows_at(row, 32)
        for dx in (2, 1, 3, 0):
            for dc in (0, 1):
                if dx or dc:
                    target = lax.rem(x + dx, 4) * 2 + lax.rem(core + dc, 2)
                    src = sent.at[0, rows_at(target, 32)]
                    send(("gx", dx, dc), src, came.at[0, mine], at(dx=dx, dc=dc))
        move(("gx", 0, 0), sent.at[0, mine], came.at[0, mine])

    def strips_col():
        got(*(("gx", dx, dc) for dx in range(4) for dc in range(2)))
        o = iota((SLOTS, SLOTS), 0)
        source = ((o >> 1) & 7) * 32 + (o >> 4) * 2 + (o & 1)
        taken = ones(iota((SLOTS, SLOTS), 1) == source)
        sent[1] = jnp.dot(taken, came[0], preferred_element_type=F32).astype(BF)
        mine = rows_at(col, 16)
        for dz in (2, 1, 3, 0):
            for dy in (2, 1, 3, 0):
                if dz or dy:
                    target = lax.rem(z + dz, 4) * 4 + lax.rem(y + dy, 4)
                    src = sent.at[1, rows_at(target, 16)]
                    send(("gc", dz, dy), src, came.at[1, mine], at(dz=dz, dy=dy))
        move(("gc", 0, 0), sent.at[1, mine], came.at[1, mine])

    def field():
        got(("patterns",))
        got(*(("gc", dz, dy) for dz in range(4) for dy in range(4)))
        tags = came[1, :, ATOM * BLK :].astype(F32)
        atom, block = tags[:, 0:1], tags[:, 1:2]
        cell = jnp.where(atom > 0.0, block * ATOMS + atom - 1.0, -1.0)
        placing = ones(iota((SLOTS, TC), 1).astype(F32) == cell)
        summed = lax.dot_general(
            placing, came[1, :, : ATOM * BLK], (((0,), (0,)), ((), ())), preferred_element_type=F32
        )
        for j in range(TC // BLK):
            for i in range(ATOM):
                placed[pl.ds(j * TR + i, ATOMS, stride=ATOM), :] = summed[
                    j * ATOMS : (j + 1) * ATOMS, i * BLK : (i + 1) * BLK
                ]

        @pl.loop(0, TR // BLK)
        def _(i):
            where = pl.ds(pl.multiple_of(i * BLK, BLK), BLK)
            for j in range(TC // BLK):
                mine = pl.ds(pl.multiple_of(z * TC + j * BLK, BLK), BLK)
                value = keep(2, i, j) * placed[pl.ds(pl.multiple_of(j * TR + i * BLK, BLK), BLK), :]
                a[1, where, mine] = (-value).astype(BF)

    move(("strips",), strips_hbm, strips)
    move(("zero",), zero_hbm, tile(0))
    move(("patterns",), patterns_hbm, patterns)
    peers = [at(dx=dx, dc=dc) for dx in range(4) for dc in range(2) if dx or dc]
    peers += [at(dz=dz, dy=dy) for dz in range(4) for dy in range(4) if dz or dy]
    peers += [at(dy=dy, dc=1) for dy in (1, 2, 3)]
    barrier = pltpu.get_barrier_semaphore()
    for peer in peers:
        pl.semaphore_signal(barrier, inc=1, device_id=peer, device_id_type=MESH)
    strips_place()
    pl.semaphore_wait(barrier, len(peers))

    side(0, 0)
    turn(0, 0)
    turn(0, 1)
    strips_x()
    side(0, 1)
    own(0, 2)
    strips_col()
    own(0, 3)
    side_on(0, 0, 3)
    own(0, 1)
    side_on(0, 1, 3)
    fwd(0, 2, 3)
    side_on(0, 0, 1)
    fwd(0, 3, 3)
    fwd(0, 3, 1)
    side_on(0, 1, 1)
    fwd(0, 2, 1)
    own(0, 0)
    field()
    turn(1, 0)
    last(0, 2, 3)
    turn(1, 1)
    last(0, 2, 1)
    fwd(0, 1, 3)
    last(0, 3, 1)
    side(1, 0)
    fwd(0, 1, 1)
    fwd(0, 0, 3)
    sq(0, 2, 0)
    send_far(0, 0)
    last(0, 3, 3)
    sq(0, 3, 0)
    free(0, 0, 3)
    side(1, 1)
    fwd(0, 0, 1)
    last(0, 1, 1)
    sq(0, 2, 1)
    send_far(0, 1)
    own(1, 3)
    own(1, 2)
    last(0, 1, 3)
    sq(0, 1, 0)
    free(0, 0, 1)
    side_on(1, 0, 3)
    dep(0, 0, 3)
    sq(0, 3, 1)
    own(1, 1)
    last(0, 0, 3)
    dep(0, 0, 1)
    sq(0, 1, 1)
    side_on(1, 0, 1)
    free(0, 1, 1)
    last(0, 0, 1)
    side_on(1, 1, 1)
    sq(0, 0, 1)
    fwd(1, 2, 1)
    fwd(1, 2, 3)
    dep(0, 1, 3)
    side_on(1, 1, 3)
    fwd(1, 3, 3)
    fwd(1, 3, 1)
    free(0, 1, 3)
    sq(0, 0, 0)
    dep(0, 1, 1)
    finish(0, 0)
    side(2, 0)
    turn(2, 0)
    last(1, 2, 3)
    cra(0, 1, 0)
    own(1, 0)
    cra(0, 2, 0)
    last(1, 2, 1)
    fwd(1, 1, 1)
    crb(0, 2, 0)
    last(1, 3, 1)
    send_far(1, 0)
    cra(0, 3, 0)
    fwd(1, 1, 3)
    finish(0, 1)
    side(2, 1)
    cra(0, 2, 1)
    fwd(1, 0, 1)
    turn(2, 1)
    last(1, 3, 3)
    crb(0, 2, 1)
    last(1, 1, 1)
    send_far(1, 1)
    last(1, 1, 3)
    cra(0, 3, 1)
    crb(0, 1, 0)
    free(1, 0, 1)
    fwd(1, 0, 3)
    crb(0, 3, 0)
    dep(1, 0, 3)
    cra(0, 1, 1)
    own(2, 2)
    side_on(2, 0, 3)
    dep(1, 0, 1)
    crb(0, 3, 1)
    last(1, 0, 1)
    free(1, 0, 3)
    side_on(2, 1, 3)
    side_on(2, 1, 1)
    cra(0, 0, 0)
    own(2, 1)
    last(1, 0, 3)
    crb(0, 1, 1)
    free(1, 1, 1)
    dep(1, 1, 1)
    side_on(2, 0, 1)
    fwd(2, 2, 1)
    own(2, 3)
    free(1, 1, 3)
    dep(1, 1, 3)
    crb(0, 0, 0)
    finish(1, 0)
    fwd(2, 2, 3)
    side(3, 0)
    cra(0, 0, 1)
    turn(3, 0)
    fwd(2, 1, 3)
    crb(0, 0, 1)
    fwd(2, 1, 1)
    fwd(2, 3, 1)
    fwd(2, 3, 3)
    last(2, 2, 1)
    last(2, 2, 3)
    finish(1, 1)
    turn(3, 1)
    side(3, 1)
    sq(1, 2, 0)
    send_far(2, 0)
    last(2, 1, 3)
    sq(1, 2, 1)
    own(2, 0)
    side_on(3, 0, 1)
    send_far(2, 1)
    last(2, 3, 1)
    side_on(3, 0, 3)
    last(2, 3, 3)
    sq(1, 3, 1)
    free(2, 1, 3)
    last(2, 1, 1)
    own(3, 2)
    own(3, 3)
    sq(1, 1, 0)
    dep(2, 0, 1)
    sq(1, 1, 1)
    side_on(3, 1, 3)
    side_on(3, 1, 1)
    sq(1, 3, 0)
    dep(2, 0, 3)
    free(2, 0, 3)
    free(2, 0, 1)
    fwd(3, 2, 3)
    fwd(3, 2, 1)
    dep(2, 1, 1)
    own(3, 1)
    dep(2, 1, 3)
    cra(1, 2, 0)
    cra(1, 1, 0)
    fwd(3, 3, 1)
    last(3, 2, 1)
    free(2, 1, 1)
    cra(1, 1, 1)
    fwd(3, 3, 3)
    last(3, 2, 3)
    fwd(2, 0, 1)
    cra(1, 2, 1)
    cra(1, 3, 1)
    fwd(3, 1, 1)
    fwd(3, 1, 3)
    fwd(2, 0, 3)
    crb(1, 2, 1)
    send_far(3, 1)
    own(3, 0)
    cra(1, 3, 0)
    last(3, 3, 1)
    crb(1, 2, 0)
    last(3, 1, 1)
    last(3, 3, 3)
    send_far(3, 0)
    last(3, 1, 3)
    crb(1, 3, 1)
    last(2, 0, 3)
    crb(1, 1, 1)
    free(3, 1, 1)
    free(3, 1, 3)
    crb(1, 3, 0)
    fwd(3, 0, 1)
    free(3, 0, 3)
    fwd(3, 0, 3)
    last(2, 0, 1)
    dep(3, 1, 1)
    crb(1, 1, 0)
    dep(3, 1, 3)
    sq(1, 0, 0)
    cra(1, 0, 1)
    dep(3, 0, 1)
    free(3, 0, 1)
    dep(3, 0, 3)
    sq(1, 0, 1)
    finish(2, 1)
    cra(1, 0, 0)
    last(3, 0, 1)
    last(3, 0, 3)
    crb(1, 0, 1)
    crb(1, 0, 0)
    finish(2, 0)
    finish(3, 1)
    finish(3, 0)

    got(*(name for name in moves if name[0] == "out"))
    gone(*copies)


def hand_on(zero, first, out_zero, out_first, held, in_sem, out_sem):
    ins, outs = [], []
    for i in range(4):
        where = pl.ds(i * SUB, SUB)
        for p, (src, dst) in enumerate(((zero, out_zero), (first, out_first))):
            n, slot = len(ins), held.at[p, where]
            ins.append(pltpu.make_async_copy(src.at[where], slot, in_sem.at[n]))
            outs.append(pltpu.make_async_copy(slot, dst.at[where], out_sem.at[n]))
            ins[n].start()
    for arrive, leave in zip(ins, outs):
        arrive.wait()
        leave.start()
    for leave in outs:
        leave.wait()


def on_device(density, strips, dest_device, atom_slot, block_slot, patterns):
    out = jax.ShapeDtypeStruct((TR, TC), F32)
    vmem = pl.BlockSpec(memory_space=pltpu.VMEM)
    hbm = pl.BlockSpec(memory_space=pl.ANY)
    results = pl.pallas_call(
        kernel,
        out_shape=(out, out),
        in_specs=[
            hbm, hbm, vmem, vmem, vmem, hbm,
        ],
        out_specs=(hbm, hbm),
        scratch_shapes=[
            pltpu.VMEM((4, TR, KB), BF),
            pltpu.VMEM((4, 4, KB, TC), BF),
            pltpu.VMEM((2, 4, TR, TC), F32),
            pltpu.VMEM((2, 3, TR, TC), BF),
            pltpu.VMEM((4, 2, TR, TC), BF),
            pltpu.VMEM((4, TR, TC), BF),
            pltpu.VMEM((ITEMS, WIDE), BF),
            pltpu.VMEM((2, SLOTS, WIDE), BF),
            pltpu.VMEM((2, SLOTS, WIDE), BF),
            pltpu.VMEM((TC // BLK * TR, BLK), F32),
            pltpu.VMEM((ITEMS * ATOM, BLK), BF),
            pltpu.SMEM((3, 48, 48), I32),
            pltpu.VMEM((2, TR, TC), F32),
            pltpu.SemaphoreType.DMA((N_COPIES,)),
            pltpu.SemaphoreType.DMA((N_COPIES,)),
            pltpu.SemaphoreType.DMA((16,)),
        ],
        compiler_params=pltpu.CompilerParams(
            collective_id=0, has_side_effects=True, vmem_limit_bytes=62 * 2**20 - 2**19
        ),
        cost_estimate=pl.CostEstimate(flops=21743271936, bytes_accessed=8 * 2**20, transcendentals=0),
    )(
        density,
        strips.reshape(ITEMS * ATOM, BLK),
        dest_device.reshape(1, ITEMS),
        atom_slot.reshape(1, ITEMS),
        block_slot.reshape(1, ITEMS),
        patterns,
    )
    return tuple(pl.pallas_call(
        hand_on,
        out_shape=(out, out),
        in_specs=(hbm, hbm),
        out_specs=(hbm, hbm),
        scratch_shapes=[
            pltpu.VMEM((2, TR, TC), F32),
            pltpu.SemaphoreType.DMA((8,)),
            pltpu.SemaphoreType.DMA((8,)),
        ],
    )(*results))


def solution(mesh):
    return jax.shard_map(
        on_device,
        mesh=mesh,
        in_specs=(
            P("row", "col"),
            P(("row", "col"), None, None),
            P(("row", "col"), None),
            P(("row", "col")),
            P(("row", "col")),
            P(),
        ),
        out_specs=(P("row", "col"), P("row", "col")),
        check_vma=False,
    )
```
